256 devices in a mesh: gx: 8 (over z), gy: 8 (over x, core), gz: 4 (over y).
Axes of the slice: x: 4, y: 4, z: 8, core: 2. Of those that a mesh axis runs over, the one named last changes fastest.
Arguments:
- velocity: float32 [2, 32, 512, 1024], P(None, 'gz', 'gx', 'gy'), may hold values from -6 to 6
- viscosity: float32 [32, 512, 1024], P('gz', 'gx', 'gy'), may hold values from 0.3 to 3
- block_inverse: float32 [3, 32, 512, 1024], P(None, 'gz', 'gx', 'gy'), may hold values from -0.05 to 1, as said below
- coupling: float32 [32, 512, 1024], P('gz', 'gx', 'gy'), may hold values from 0.85 to 1
- friction: float32 [512, 1024], P('gx', 'gy'), may hold values from 0.5 to 5
- friction_step: float32 [512, 1024], P('gx', 'gy'), may hold values from -6 to 6
- misfit_weight: float32 [512, 1024], P('gx', 'gy'), may hold values from 0.5 to 2
- ice_tiles: int32 [32, 64], P('gx', 'gy'), may hold values 0 or 1
- bed_layer: int32 [512, 1024], P('gx', 'gy'), may hold values from 0 to 30
Outputs:
- increment: float32 [2, 32, 512, 1024], P(None, 'gz', 'gx', 'gy')
- adjoint: float32 [2, 32, 512, 1024], P(None, 'gz', 'gx', 'gy')
- hessian_action: float32 [512, 1024], P('gx', 'gy')
The draws below stay inside these ranges and needn't reach their ends.
Inputs may be any that keep to these rules, and one draw needn't show every extreme that they name: For every cell the block [[block_inverse[0], block_inverse[1]], [block_inverse[1], block_inverse[2]]] is symmetric positive definite, its diagonal entries at least 0.85 and its off-diagonal entry at most 0.05 in magnitude.
All inputs are finite; a program needn't handle non-finite values. No bound on the sum of `ice_tiles` on one device may be relied on, other than what follows from the above.
Results may differ from the reference program's by a relative error of at most 0.0001.
Values sent between devices are 32-bit elements; how exact they have to be, the bound alone decides.
A program may use at most 64 MiB of HBM per device.

```python
import math
import jax
import jax.numpy as jnp
from jax import lax

TILE = 16
ITERS = 2
NX = 512
NY = 1024
NZ = 32


def draw_block_inverse(key, part):
    first_key, second_key, third_key = jax.random.split(key, 3)
    grid_shape = (NZ, NX, NY)
    leading = jax.random.uniform(first_key, grid_shape, jnp.float32, 0.88, 0.98)
    trailing = jax.random.uniform(second_key, grid_shape, jnp.float32, 0.88, 0.98)
    crossing = jax.random.uniform(third_key, grid_shape, jnp.float32, -0.04, 0.04)
    return jnp.stack([leading, crossing, trailing]).astype(jnp.float32)


def plant(values, rng, least, high):
    spot = [jax.random.randint(jax.random.fold_in(rng, axis), (), 0, length) for axis, length in enumerate(values.shape)]
    widest = values.shape.index(max(values.shape))
    neighbour = spot[:widest] + [(spot[widest] + 1) % values.shape[widest]] + spot[widest + 1:]
    return values.at[tuple(spot)].set(least).at[tuple(neighbour)].set(high)


def block_levels(rng, extent, cuts, low, high):
    gain = 1.0
    for dim, parts in cuts:
        heights = jax.random.uniform(jax.random.fold_in(jax.random.fold_in(rng, 6), dim), (parts,), jnp.float32, low / len(cuts), high / len(cuts))
        gain = gain * jnp.repeat(jnp.exp(heights), extent[dim] // parts).reshape((-1,) + (1,) * (len(extent) - 1 - dim))
    return gain


def normal_values(own_key, shape, scale, reach, shards=(), kind=jnp.bfloat16):
    values = scale * jax.random.normal(own_key, shape, jnp.float32)
    if shards:
        values = values * block_levels(own_key, shape, shards, -0.22, 0.18)
    return jnp.clip(values, -reach, reach).astype(kind)


def setup_inputs(seed: int = 0) -> dict:
    streams_of = jax.random.split(jax.random.key(seed), 10)
    return {
        "velocity": normal_values(streams_of[0], (2, NZ, NX, NY), 1.0, 6.0, ((1, 4), (2, 8), (3, 8)), jnp.float32),
        "viscosity": jnp.clip(jnp.exp(math.log(3.0) - 2.3025851 * jax.random.uniform(streams_of[1], (NZ, NX, NY), jnp.float32) ** block_levels(streams_of[1], (NZ, NX, NY), ((0, 4), (1, 8), (2, 8)), -0.2, 0.2)), 0.3, 3.0),
        "block_inverse": draw_block_inverse(jax.random.fold_in(streams_of[9], 71), 0),
        "coupling": jnp.clip(0.85 + 0.14999998 * jax.random.uniform(streams_of[3], (NZ, NX, NY), jnp.float32) ** block_levels(streams_of[3], (NZ, NX, NY), ((0, 4), (1, 8), (2, 8)), -0.2, 0.2), 0.85, 1.0),
        "friction": jnp.clip(jnp.exp(math.log(5.0) - 2.3025851 * jax.random.uniform(streams_of[4], (NX, NY), jnp.float32) ** block_levels(streams_of[4], (NX, NY), ((0, 8), (1, 8)), -0.2, 0.2)), 0.5, 5.0),
        "friction_step": normal_values(streams_of[5], (NX, NY), 1.0, 6.0, ((0, 8), (1, 8)), jnp.float32),
        "misfit_weight": jnp.clip(jnp.exp(math.log(2.0) - 1.3862944 * jax.random.uniform(streams_of[6], (NX, NY), jnp.float32) ** block_levels(streams_of[6], (NX, NY), ((0, 8), (1, 8)), -0.2, 0.2)), 0.5, 2.0),
        "ice_tiles": plant((jax.random.randint(streams_of[7], (NX // TILE, NY // TILE), 0, 5) < 4).astype(jnp.int32), jax.random.fold_in(streams_of[7], 1), 0, 1),
        "bed_layer": plant(jax.random.randint(streams_of[8], (NX, NY), 0, NZ - 1), jax.random.fold_in(streams_of[8], 1), 0, (NZ - 1) - 1).astype(jnp.int32),
    }


VERTICAL = 8.0
STRETCH = 4.0


def expand_tiles(ice_tiles):
    column = jnp.repeat(jnp.repeat(ice_tiles, TILE, axis=0), TILE, axis=1)
    return column.astype(jnp.float32)


def neighbor_slices():
    inner = slice(1, -1)
    return [(slice(2, None), inner, inner), (slice(None, -2), inner, inner),
            (inner, slice(2, None), inner), (inner, slice(None, -2), inner),
            (inner, inner, slice(2, None)), (inner, inner, slice(None, -2))]


def face_weights(padded_eta, padded_act):
    centre = (slice(1, -1), slice(1, -1), slice(1, -1))
    centre_eta = padded_eta[centre]
    centre_act = padded_act[centre]
    result = []
    for position, slices in enumerate(neighbor_slices()):
        factor = VERTICAL if position < 2 else 1.0
        result.append(factor * 0.5 * (centre_eta + padded_eta[slices]) * centre_act * padded_act[slices])
    return result


def apply_operator(field, weights, diagonal):
    padded = jnp.pad(field, ((0, 0), (1, 1), (1, 1), (1, 1)))
    stretch_x = jnp.array([STRETCH, 1.0], jnp.float32).reshape(2, 1, 1, 1)
    stretch_y = jnp.array([1.0, STRETCH], jnp.float32).reshape(2, 1, 1, 1)
    nbrs = [padded[(slice(None),) + slices] for slices in neighbor_slices()]
    vertical = weights[0] * nbrs[0] + weights[1] * nbrs[1]
    east_west = weights[2] * nbrs[2] + weights[3] * nbrs[3]
    north_south = weights[4] * nbrs[4] + weights[5] * nbrs[5]
    return diagonal * field - vertical - stretch_x * east_west - stretch_y * north_south


def precondition(residual, inverse, coupled):
    def rising(incoming, layer):
        source, block, link = layer
        total = source + link * incoming
        value = jnp.stack([block[0] * total[0] + block[1] * total[1], block[1] * total[0] + block[2] * total[1]])
        return value, value

    start = jnp.zeros(residual.shape[:1] + residual.shape[2:], jnp.float32)
    inverse_layers = jnp.moveaxis(inverse, 1, 0)
    _, upward = lax.scan(rising, start, (jnp.moveaxis(residual, 1, 0), inverse_layers, coupled))

    def falling(incoming, layer):
        value_up, block, link = layer
        value = value_up + jnp.stack([block[0] * incoming[0] + block[1] * incoming[1], block[1] * incoming[0] + block[2] * incoming[1]])
        return link * value, value

    _, downward = lax.scan(falling, start, (upward, inverse_layers, coupled), reverse=True)
    return jnp.moveaxis(downward, 0, 1)


def solve(rhs, operator, precond_fn):
    solution = jnp.zeros_like(rhs)
    residual = rhs
    precond = precond_fn(residual)
    direction = precond
    energy = jnp.sum(residual * precond)
    for iteration in range(ITERS):
        image = operator(direction)
        step_length = energy / jnp.sum(direction * image)
        solution = solution + step_length * direction
        residual = residual - step_length * image
        if iteration + 1 < ITERS:
            precond = precond_fn(residual)
            renewed = jnp.sum(residual * precond)
            direction = precond + (renewed / energy) * direction
            energy = renewed
    return solution


def reference(velocity, viscosity, block_inverse, coupling, friction, friction_step, misfit_weight, ice_tiles, bed_layer):
    column = expand_tiles(ice_tiles)
    levels = jnp.arange(NZ, dtype=jnp.int32).reshape(NZ, 1, 1)
    active = column[None] * (levels >= bed_layer[None]).astype(jnp.float32)
    beneath = column[None] * (levels - 1 >= bed_layer[None]).astype(jnp.float32)
    bedflag = column[None] * (levels == bed_layer[None]).astype(jnp.float32)
    surface = column[None] * (levels == NZ - 1).astype(jnp.float32)
    padded_eta = jnp.pad(viscosity, 1)
    padded_act = jnp.pad(active, 1)
    weights = face_weights(padded_eta, padded_act)
    stretch_x = jnp.array([STRETCH, 1.0], jnp.float32).reshape(2, 1, 1, 1)
    stretch_y = jnp.array([1.0, STRETCH], jnp.float32).reshape(2, 1, 1, 1)
    diagonal = (weights[0] + weights[1]) + stretch_x * (weights[2] + weights[3]) + stretch_y * (weights[4] + weights[5]) + friction * bedflag + (1.0 - active)
    inverse = jnp.stack([active * block_inverse[0] + (1.0 - active), active * block_inverse[1], active * block_inverse[2] + (1.0 - active)])
    coupled = coupling * active * beneath

    def operator(field):
        return apply_operator(field, weights, diagonal)

    def precond_fn(field):
        return precondition(field, inverse, coupled)

    increment = solve(bedflag * friction * friction_step * velocity, operator, precond_fn)
    adjoint = solve(surface * misfit_weight * increment, operator, precond_fn)
    hessian_action = friction * jnp.sum(bedflag * velocity * adjoint, axis=(0, 1))
    return increment, adjoint, hessian_action
```

```python
import functools

import jax
import jax.numpy as jnp
from jax import lax
from jax.experimental import pallas as pl
from jax.experimental.pallas import tpu as pltpu
from jax.sharding import PartitionSpec as P

TILE = 16
VERTICAL = 8.0
STRETCH = 4.0
NONE = 1000.0
MESH = pl.DeviceIdType.MESH
F32 = jnp.float32
NZ = 32
ROWS = 16
LANES = 128
UNROLL = 4


def blocked_loop(steps, body, carry):
    def chunk(index, state):
        for inner in range(UNROLL):
            state = body(index * UNROLL + inner, state)
        return state

    return lax.fori_loop(0, steps // UNROLL, chunk, carry)


def kernel(
    sizes,
    vel, visc, binv, coup, fric, fstep, misfit, ice, bed,
    inc, adj, hess,
    V, B, L, vbs, vbp, WU, WE, WW, WN, WS, D0, D1,
    Z0, ZA, S0, SA, ZB, SB,
    xs0, xr0, ps0, pr0, xs1, xr1, ps1, pr1, xs2, xr2, ps2, pr2, xs3, xr3, ps3, pr3,
    rt, ra, rb,
    loc_sem, in_send, in_recv, halo_send, halo_recv, red_send, red_recv_a, red_recv_b,
    out_send, out_recv,
):
    ngx, ngy, ngz = sizes
    gx, gy, gz = lax.axis_index("gx"), lax.axis_index("gy"), lax.axis_index("gz")
    depth = NZ // ngz
    odd = gx % 2

    def piece_of(q):
        return q + odd * (ngz - 1 - 2 * q)

    piece = piece_of(gz)
    total_pieces = ngx * ngz
    spot = gx * ngz + piece

    def holder(index):
        block = index // ngz
        part = index % ngz
        return (block, gy, part + (block % 2) * (ngz - 1 - 2 * part))

    x_low = holder((spot + total_pieces - 1) % total_pieces)
    x_high = holder((spot + 1) % total_pieces)
    y_low = (gx, (gy + ngy - 1) % ngy, gz)
    y_high = (gx, (gy + 1) % ngy, gz)
    peers = [(gx, gy, (gz + o) % ngz) for o in range(1, ngz)]
    half = ngz // 2
    na, nb = ngx * 2, ngy * half
    ma, mb = gx * 2 + gz % 2, gy * half + gz // 2

    def member_a(o):
        m = (ma + o) % na
        return (m // 2, gy, (gz // 2) * 2 + m % 2)

    def member_b(o):
        m = (mb + o) % nb
        return (gx, m // half, (m % half) * 2 + gz % 2)

    group_a = [member_a(o) for o in range(1, na)]
    group_b = [member_b(o) for o in range(1, nb)]

    barrier = pltpu.get_barrier_semaphore()
    partners = [x_low, x_high, y_low, y_high] + peers + group_a + group_b
    for partner in partners:
        pl.semaphore_signal(barrier, inc=1, device_id=partner, device_id_type=MESH)

    base = gz * depth
    bedf = bed[...]
    vb0 = jnp.zeros(bedf.shape, F32)
    vb1 = jnp.zeros(bedf.shape, F32)
    for k in range(depth):
        at = bedf == base + k
        vb0 = jnp.where(at, vel[0, k], vb0)
        vb1 = jnp.where(at, vel[1, k], vb1)
    vbs[0] = vb0
    vbs[1] = vb1

    pl.semaphore_wait(barrier, len(partners))

    here = pl.multiple_of(piece * ROWS, ROWS)
    layers = pl.ds(base, depth)

    def moves(part, o):
        rows = pl.ds(pl.multiple_of(part * ROWS, ROWS), ROWS)
        return [
            (visc.at[:, rows, :], V.at[layers]),
            (binv.at[:, :, rows, :], B.at[:, layers]),
            (coup.at[:, rows, :], L.at[layers]),
            (vbs.at[:, rows, :], vbp.at[o]),
        ]

    locals_in = []
    for a, (src, dst) in enumerate(moves(piece, 0)):
        copy = pltpu.make_async_copy(src, dst, loc_sem.at[a])
        copy.start()
        locals_in.append(copy)
    incoming = [[], [], [], []]
    per_peer = [moves(piece_of((gz + o) % ngz), o) for o in range(1, ngz)]
    for a in range(4):
        for o in range(1, ngz):
            src, dst = per_peer[o - 1][a]
            copy = pltpu.make_async_remote_copy(
                src_ref=src, dst_ref=dst,
                send_sem=in_send.at[a, o], recv_sem=in_recv.at[a, o],
                device_id=peers[o - 1], device_id_type=MESH,
            )
            copy.start()
            incoming[a].append(copy)

    row = lax.broadcasted_iota(jnp.int32, (ROWS, LANES), 0)
    lane = lax.broadcasted_iota(jnp.int32, (ROWS, LANES), 1)
    column = jnp.zeros((ROWS, LANES), F32)
    for j in range(LANES // TILE):
        flag = ice[piece, j].astype(F32)
        column = jnp.where(lane // TILE == j, flag, column)
    has_ice = column > 0.5
    my_rows = pl.ds(here, ROWS)
    kbed = jnp.where(has_ice, bed[my_rows, :].astype(F32), NONE)
    friction = fric[my_rows, :]
    load = misfit[my_rows, :] * column

    for field in (Z0, ZA, S0, SA, ZB, SB):
        for c in range(2):
            field[c, 0] = jnp.zeros((ROWS, LANES), F32)
            field[c, NZ + 1] = jnp.zeros((ROWS, LANES), F32)
    for ps in (ps0, ps3):
        ps[...] = jnp.zeros(ps.shape, F32)

    def pack_lane(packed, value, j):
        low, high = packed
        low = jnp.where(lane == j, pltpu.roll(value, j, 1), low)
        high = jnp.where(lane == j, pltpu.roll(value, (j + 1) % LANES, 1), high)
        return low, high

    def pack_rows(xs, value, j):
        xs[0, pl.ds(j, 1), :] = value[0:1, :]
        xs[1, pl.ds(j, 1), :] = value[ROWS - 1 : ROWS, :]

    def send_halo(index, xs, xr, ps, pr):
        copies = []
        for side, (src, dst, device) in enumerate(
            [
                (ps.at[0], pr.at[1], y_low),
                (ps.at[1], pr.at[0], y_high),
                (xs.at[0], xr.at[1], x_low),
                (xs.at[1], xr.at[0], x_high),
            ]
        ):
            copy = pltpu.make_async_remote_copy(
                src_ref=src, dst_ref=dst,
                send_sem=halo_send.at[index, side], recv_sem=halo_recv.at[index, side],
                device_id=device, device_id_type=MESH,
            )
            copy.start()
            copies.append(copy)
        return copies

    def beside(value, xr, xj, left, right, lj):
        east = jnp.where(row == ROWS - 1, xr[1, pl.ds(xj, 1), :], pltpu.roll(value, ROWS - 1, 0))
        west = jnp.where(row == 0, xr[0, pl.ds(xj, 1), :], pltpu.roll(value, 1, 0))
        north = jnp.where(
            lane == LANES - 1, pltpu.roll(right, LANES - 1 - lj, 1), pltpu.roll(value, LANES - 1, 1)
        )
        south = jnp.where(
            lane == 0, pltpu.roll(left, (LANES - lj) % LANES, 1), pltpu.roll(value, 1, 1)
        )
        return east, west, north, south

    locals_in[0].wait()
    for copy in incoming[0]:
        copy.wait_recv()

    def pack_viscosity(k, packed):
        value = V[k]
        pack_rows(xs0, value, k)
        return pack_lane(packed, value, k)

    blank = jnp.zeros((ROWS, LANES), F32)
    packed = blocked_loop(NZ, pack_viscosity, (blank, blank))
    pack_rows(xs0, kbed, NZ)
    low, high = pack_lane(packed, kbed, NZ)
    ps0[0] = low
    ps0[1] = high
    halo0 = send_halo(0, xs0, xr0, ps0, pr0)

    for copy in halo0:
        copy.wait_recv()
    left, right = pr0[0], pr0[1]
    bed_e, bed_w, bed_n, bed_s = beside(kbed, xr0, NZ, left, right, NZ)
    bed_e = jnp.where((row == ROWS - 1) & (spot == total_pieces - 1), NONE, bed_e)
    bed_w = jnp.where((row == 0) & (spot == 0), NONE, bed_w)
    bed_n = jnp.where((lane == LANES - 1) & (gy == ngy - 1), NONE, bed_n)
    bed_s = jnp.where((lane == 0) & (gy == 0), NONE, bed_s)

    def layer_weights(k, carry):
        below_v, below_a = carry
        level = jnp.full((ROWS, LANES), k, jnp.int32).astype(F32)
        value = V[k]
        act = jnp.where(level >= kbed, 1.0, 0.0)
        bedflag = jnp.where(level == kbed, 1.0, 0.0)
        east, west, north, south = beside(value, xr0, k, left, right, k)
        half_act = 0.5 * act
        down = (VERTICAL * (value + below_v)) * (half_act * below_a)
        we = (value + east) * jnp.where(level >= bed_e, half_act, 0.0)
        ww = (value + west) * jnp.where(level >= bed_w, half_act, 0.0)
        wn = (value + north) * jnp.where(level >= bed_n, half_act, 0.0)
        ws = (value + south) * jnp.where(level >= bed_s, half_act, 0.0)
        WU[k] = down
        WE[k] = we
        WW[k] = ww
        WN[k] = wn
        WS[k] = ws
        ew, ns = we + ww, wn + ws
        rest = friction * bedflag + (1.0 - act)
        D0[k] = down + STRETCH * ew + ns + rest
        D1[k] = down + ew + STRETCH * ns + rest
        return value, act

    blocked_loop(NZ, layer_weights, (blank, blank))
    WU[NZ] = blank

    for group, copy in zip(incoming[1:], locals_in[1:]):
        copy.wait()
        for remote in group:
            remote.wait_recv()
    speed0 = vbp[0, 0]
    speed1 = vbp[0, 1]
    for o in range(1, ngz):
        speed0 = speed0 + vbp[o, 0]
        speed1 = speed1 + vbp[o, 1]
    speed0 = jnp.where(has_ice, speed0, 0.0)
    speed1 = jnp.where(has_ice, speed1, 0.0)
    drive = friction * fstep[my_rows, :]
    push0, push1 = drive * speed0, drive * speed1

    def apply_inverse(k, first, second):
        b0, b1, b2 = B[0, k], B[1, k], B[2, k]
        return b0 * first + b1 * second, b1 * first + b2 * second

    def rise(k, first, second, state, out):
        y0, y1, total = state
        link = L[k]
        t0 = first + link * y0
        t1 = second + link * y1
        y0, y1 = apply_inverse(k, t0, t1)
        out[0, k + 1] = y0
        out[1, k + 1] = y1
        return y0, y1, total + (t0 * y0 + t1 * y1)

    def first_rise(k, state):
        level = jnp.full((ROWS, LANES), k, jnp.int32).astype(F32)
        act = jnp.where(level >= kbed, 1.0, 0.0)
        beneath = jnp.where(level - 1.0 >= kbed, 1.0, 0.0)
        rest = 1.0 - act
        B[0, k] = act * B[0, k] + rest
        B[1, k] = act * B[1, k]
        B[2, k] = act * B[2, k] + rest
        L[k] = L[k] * act * beneath
        at = level == kbed
        first = jnp.where(at, push0, 0.0)
        second = jnp.where(at, push1, 0.0)
        above = WU[k + 1]
        D0[k] = D0[k] + above
        D1[k] = D1[k] + above
        return rise(k, first, second, state, Z0)

    state = blocked_loop(NZ, first_rise, (blank, blank, blank))
    rz0 = state[2]

    def fall(k, g0, g1, field):
        add0, add1 = apply_inverse(k, g0, g1)
        z0 = field[0, k + 1] + add0
        z1 = field[1, k + 1] + add1
        field[0, k + 1] = z0
        field[1, k + 1] = z1
        link = L[k]
        return z0, z1, link * z0, link * z1

    def fall_bare(k, g0, g1, field):
        z0, z1 = apply_inverse(k, g0, g1)
        field[0, k + 1] = z0
        field[1, k + 1] = z1
        link = L[k]
        return z0, z1, link * z0, link * z1

    seed_a0, seed_a1 = load * Z0[0, NZ], load * Z0[1, NZ]

    def fall_first(i, carry):
        k = NZ - 1 - i
        g0, g1, a0, a1, low, high = carry
        z0, z1, g0, g1 = fall(k, g0, g1, Z0)
        y0, y1, a0, a1 = fall_bare(k, a0, a1, ZA)
        packed = (low, high)
        for n, value in enumerate((z0, z1, y0, y1)):
            pack_rows(xs1, value, k + NZ * n)
            packed = pack_lane(packed, value, k + NZ * n)
        return (g0, g1, a0, a1) + packed

    carry = blocked_loop(NZ, fall_first, (blank, blank, seed_a0, seed_a1, blank, blank))
    ps1[0] = carry[4]
    ps1[1] = carry[5]
    halo1 = send_halo(1, xs1, xr1, ps1, pr1)
    raa = seed_a0 * ZA[0, NZ] + seed_a1 * ZA[1, NZ]

    def operate(k, weights, field, xr, xj, left, right, lj):
        up, down, we, ww, wn, ws, d0, d1 = weights
        result = []
        for c in range(2):
            value = field[c, k + 1]
            east, west, north, south = beside(
                value, xr, xj + c * NZ + k, left, right, lj + c * NZ + k
            )
            vertical = up * field[c, k + 2] + down * field[c, k]
            ew = we * east + ww * west
            ns = wn * north + ws * south
            if c == 0:
                result.append(d0 * value - vertical - STRETCH * ew - ns)
            else:
                result.append(d1 * value - vertical - ew - STRETCH * ns)
        return result

    def weights_of(k):
        return WU[k + 1], WU[k], WE[k], WW[k], WN[k], WS[k], D0[k], D1[k]

    def against(field, k, image, total):
        return total + (field[0, k + 1] * image[0] + field[1, k + 1] * image[1])

    for copy in halo1:
        copy.wait_recv()
    left1, right1 = pr1[0], pr1[1]

    def middle_rise(k, carry):
        pq0, paa, main, extra = carry
        weights = weights_of(k)
        w = operate(k, weights, Z0, xr1, 0, left1, right1, 0)
        wa = operate(k, weights, ZA, xr1, 2 * NZ, left1, right1, 2 * NZ)
        pq0 = against(Z0, k, w, pq0)
        paa = against(ZA, k, wa, paa)
        main = rise(k, w[0], w[1], main, S0)
        extra = rise(k, wa[0], wa[1], extra, SA)
        return pq0, paa, main, extra

    triple = (blank, blank, blank)
    pq0, paa, main, extra = blocked_loop(NZ, middle_rise, (blank, blank, triple, triple))
    g0, gaa = main[2], extra[2]
    seed_b0, seed_b1 = load * S0[0, NZ], load * S0[1, NZ]

    def fall_second(i, carry):
        k = NZ - 1 - i
        g0, g1, h0, h1, b0, b1, low1, high1, low2, high2 = carry
        z0, z1, g0, g1 = fall(k, g0, g1, S0)
        a0, a1, h0, h1 = fall(k, h0, h1, SA)
        y0, y1, b0, b1 = fall_bare(k, b0, b1, ZB)
        packed = (low1, high1)
        for n, value in enumerate((y0, y1, z0, z1)):
            pack_rows(xs2, value, k + NZ * n)
            packed = pack_lane(packed, value, k + NZ * n)
        other = (low2, high2)
        for n, value in enumerate((a0, a1)):
            pack_rows(xs2, value, k + NZ * (n + 4))
            other = pack_lane(other, value, k + NZ * n)
        return (g0, g1, h0, h1, b0, b1) + packed + other

    carry = blocked_loop(
        NZ, fall_second, (blank, blank, blank, blank, seed_b0, seed_b1, blank, blank, blank, blank)
    )
    for n in range(2):
        ps2[0, ROWS * n : ROWS * (n + 1), :] = carry[6 + 2 * n]
        ps2[1, ROWS * n : ROWS * (n + 1), :] = carry[7 + 2 * n]
    halo2 = send_halo(2, xs2, xr2, ps2, pr2)
    rab = seed_a0 * ZB[0, NZ] + seed_a1 * ZB[1, NZ]
    rbb = seed_b0 * ZB[0, NZ] + seed_b1 * ZB[1, NZ]

    for copy in halo2:
        copy.wait_recv()
    left2, right2 = pr2[0, :ROWS, :], pr2[1, :ROWS, :]
    left3, right3 = pr2[0, ROWS:, :], pr2[1, ROWS:, :]

    def last_rise(k, carry):
        pab, pbb, gab, main = carry
        w = operate(k, weights_of(k), ZB, xr2, 0, left2, right2, 0)
        pab = against(ZA, k, w, pab)
        pbb = against(ZB, k, w, pbb)
        gab = against(SA, k, w, gab)
        main = rise(k, w[0], w[1], main, SB)
        return pab, pbb, gab, main

    pab, pbb, gab, main = blocked_loop(NZ, last_rise, (blank, blank, blank, triple))
    gbb = main[2]

    def fall_third(i, carry):
        k = NZ - 1 - i
        g0, g1, low, high = carry
        z0, z1, g0, g1 = fall(k, g0, g1, SB)
        packed = (low, high)
        for n, value in enumerate((z0, z1)):
            pack_rows(xs3, value, k + NZ * n)
            packed = pack_lane(packed, value, k + NZ * n)
        return (g0, g1) + packed

    carry = blocked_loop(NZ, fall_third, (blank, blank, blank, blank))
    ps3[0] = carry[2]
    ps3[1] = carry[3]
    halo3 = send_halo(3, xs3, xr3, ps3, pr3)

    def early_energy(k, carry):
        d0, daa = carry
        weights = weights_of(k)
        w = operate(k, weights, S0, xr2, 2 * NZ, left2, right2, 2 * NZ)
        wa = operate(k, weights, SA, xr2, 4 * NZ, left3, right3, 0)
        return against(S0, k, w, d0), against(SA, k, wa, daa)

    d0, daa = blocked_loop(NZ, early_energy, (blank, blank))

    for copy in halo3:
        copy.wait_recv()
    left4, right4 = pr3[0], pr3[1]

    def late_energy(k, carry):
        dab, dbb = carry
        w = operate(k, weights_of(k), SB, xr3, 0, left4, right4, 0)
        return against(SA, k, w, dab), against(SB, k, w, dbb)

    dab, dbb = blocked_loop(NZ, late_energy, (blank, blank))

    sums = [rz0, pq0, g0, d0, raa, rab, rbb, paa, pab, pbb, gaa, gab, gbb, daa, dab, dbb]
    for n, value in enumerate(sums):
        rt[0, n : n + 1, :] = jnp.sum(value, axis=0, keepdims=True)
    reductions = []
    for turn, (group, received, sem) in enumerate(((group_a, ra, red_recv_a), (group_b, rb, red_recv_b))):
        copies = []
        for o, device in enumerate(group):
            copy = pltpu.make_async_remote_copy(
                src_ref=rt.at[turn], dst_ref=received.at[o],
                send_sem=red_send.at[turn, o], recv_sem=sem.at[o],
                device_id=device, device_id_type=MESH,
            )
            copy.start()
            copies.append(copy)
        total = rt[turn]
        for o, copy in enumerate(copies):
            copy.wait_recv()
            total = total + received[o]
        if turn == 0:
            rt[1] = total
        reductions += copies
    totals = jnp.broadcast_to(jnp.sum(total, axis=1, keepdims=True), (ROWS, LANES))
    (rz0, pq0, g0, d0, raa, rab, rbb, paa, pab, pbb, gaa, gab, gbb, daa, dab, dbb) = [
        totals[n : n + 1, :] for n in range(16)
    ]

    def combination(rz, pq, g, d):
        step = rz / pq
        renewed = step * step * g - rz
        grow = 1.0 + renewed / rz
        energy = grow * grow * pq - 2.0 * grow * step * g + step * step * d
        second = renewed / energy
        return step + second * grow, -(second * step)

    c0, c1 = combination(rz0, pq0, g0, d0)

    def form(aa, ab, bb):
        return c0 * c0 * aa + 2.0 * (c0 * c1) * ab + c1 * c1 * bb

    e0, e1 = combination(form(raa, rab, rbb), form(paa, pab, pbb), form(gaa, gab, gbb), form(daa, dab, dbb))
    f_za, f_zb, f_sa, f_sb = e0 * c0, e0 * c1, e1 * c0, e1 * c1

    def results(k, carry):
        level = jnp.full((ROWS, LANES), k, jnp.int32).astype(F32)
        at = level == kbed
        out = []
        for c in range(2):
            Z0[c, k + 1] = c0 * Z0[c, k + 1] + c1 * S0[c, k + 1]
            value = (f_za * ZA[c, k + 1] + f_zb * ZB[c, k + 1]) + (f_sa * SA[c, k + 1] + f_sb * SB[c, k + 1])
            ZA[c, k + 1] = value
            out.append(jnp.where(at, value, carry[c]))
        return tuple(out)

    basal = blocked_loop(NZ, results, (blank, blank))
    action = friction * (speed0 * basal[0] + speed1 * basal[1])
    hess[my_rows, :] = action
    vbs[0, my_rows, :] = action

    finals = []
    rest = []
    back = (inc.at[:, :, my_rows, :], adj.at[:, :, my_rows, :], hess.at[my_rows, :])
    for n, field in enumerate((Z0, ZA)):
        copy = pltpu.make_async_copy(field.at[:, pl.ds(1 + base, depth)], back[n], loc_sem.at[n])
        copy.start()
        finals.append(copy)
    for o in range(1, ngz):
        theirs = pl.ds(1 + ((gz + o) % ngz) * depth, depth)
        for n, src in enumerate((Z0.at[:, theirs], ZA.at[:, theirs], vbs.at[0, my_rows, :])):
            copy = pltpu.make_async_remote_copy(
                src_ref=src, dst_ref=back[n],
                send_sem=out_send.at[n, o], recv_sem=out_recv.at[n, o],
                device_id=peers[o - 1], device_id_type=MESH,
            )
            copy.start()
            rest.append(copy)
    for copy in finals:
        copy.wait()
    for copy in rest:
        copy.wait()
    for group in incoming:
        for copy in group:
            copy.wait_send()
    for copy in halo0 + halo1 + halo2 + halo3 + reductions:
        copy.wait_send()


def local(sizes, *args):
    ngx, ngy, ngz = sizes
    field = pltpu.VMEM((NZ, ROWS, LANES), F32)
    state = pltpu.VMEM((2, NZ + 2, ROWS, LANES), F32)
    depth, rows, lanes = args[1].shape
    dma = pltpu.SemaphoreType.DMA

    def halo(length, packs):
        return [pltpu.VMEM((2, length, LANES), F32)] * 2 + [pltpu.VMEM((2, packs * ROWS, LANES), F32)] * 2

    na, nb = ngx * 2, ngy * (ngz // 2)
    scratch = (
        [field, pltpu.VMEM((3, NZ, ROWS, LANES), F32), field]
        + [pltpu.VMEM((2, rows, lanes), F32), pltpu.VMEM((ngz, 2, ROWS, LANES), F32)]
        + [pltpu.VMEM((NZ + 1, ROWS, LANES), F32)]
        + [field] * 6
        + [state] * 6
        + halo(NZ + 8, 1) + halo(4 * NZ, 1) + halo(6 * NZ, 2) + halo(2 * NZ, 1)
        + [pltpu.VMEM((2, ROWS, LANES), F32)]
        + [pltpu.VMEM((na - 1, ROWS, LANES), F32), pltpu.VMEM((nb - 1, ROWS, LANES), F32)]
        + [dma((4,)), dma((4, ngz)), dma((4, ngz)), dma((4, 4)), dma((4, 4))]
        + [dma((2, max(na, nb))), dma((na,)), dma((nb,)), dma((3, ngz)), dma((3, ngz))]
    )
    vmem = pl.BlockSpec(memory_space=pltpu.VMEM)
    hbm = pl.BlockSpec(memory_space=pl.ANY)
    smem = pl.BlockSpec(memory_space=pltpu.SMEM)
    return pl.pallas_call(
        functools.partial(kernel, sizes),
        out_shape=(
            jax.ShapeDtypeStruct((2, depth, rows, lanes), F32),
            jax.ShapeDtypeStruct((2, depth, rows, lanes), F32),
            jax.ShapeDtypeStruct((rows, lanes), F32),
        ),
        in_specs=[vmem, hbm, hbm, hbm, vmem, vmem, vmem, smem, vmem],
        out_specs=(hbm, hbm, vmem),
        scratch_shapes=scratch,
        compiler_params=pltpu.CompilerParams(
            collective_id=0, has_side_effects=True, vmem_limit_bytes=40 * 1024 * 1024
        ),
    )(*args)


def solution(mesh):
    sizes = (mesh.shape["gx"], mesh.shape["gy"], mesh.shape["gz"])
    wide, cell, flat = P(None, "gz", "gx", "gy"), P("gz", "gx", "gy"), P("gx", "gy")
    return jax.shard_map(
        functools.partial(local, sizes),
        mesh=mesh,
        in_specs=(wide, cell, wide, cell, flat, flat, flat, flat, flat),
        out_specs=(wide, wide, flat),
        check_vma=False,
    )
```

```python
import functools

import jax
import jax.numpy as jnp
from jax import lax
from jax.experimental import pallas as pl
from jax.experimental.pallas import tpu as pltpu
from jax.sharding import PartitionSpec as P

TILE = 16
VERTICAL = 8.0
STRETCH = 4.0
NONE = 1000.0
MESH = pl.DeviceIdType.MESH
F32 = jnp.float32
NZ = 32
ROWS = 16
LANES = 128
UNROLL = 8


def blocked_loop(steps, body, carry):
    def chunk(index, state):
        for inner in range(UNROLL):
            state = body(index * UNROLL + inner, state)
        return state

    return lax.fori_loop(0, steps // UNROLL, chunk, carry)


def kernel(
    sizes,
    vel_in, visc, binv, coup, fric_in, fstep_in, misfit_in, ice, bed_in,
    inc, adj, hess,
    vel, bed, fric, fstep, misfit,
    V, B, L, vbs, vbp, WU, WE, WW, WN, WS, D0, D1,
    Z0, ZA, S0, SA, ZB, SB,
    xs0, xr0, ps0, pr0, xs1, xr1, ps1, pr1, xs2, xr2, ps2, pr2, xs3, xr3, ps3, pr3,
    stack, rt, ra, rb,
    load_sem, loc_sem, in_send, in_recv, halo_send, halo_recv, red_send, red_recv_a, red_recv_b,
    out_send, out_recv,
):
    ngx, ngy, ngz = sizes
    gx, gy, gz = lax.axis_index("gx"), lax.axis_index("gy"), lax.axis_index("gz")
    depth = NZ // ngz
    odd = gx % 2

    def piece_of(q):
        return q + odd * (ngz - 1 - 2 * q)

    piece = piece_of(gz)
    total_pieces = ngx * ngz
    spot = gx * ngz + piece

    def holder(index):
        block = index // ngz
        part = index % ngz
        return (block, gy, part + (block % 2) * (ngz - 1 - 2 * part))

    x_low = holder((spot + total_pieces - 1) % total_pieces)
    x_high = holder((spot + 1) % total_pieces)
    y_low = (gx, (gy + ngy - 1) % ngy, gz)
    y_high = (gx, (gy + 1) % ngy, gz)
    peers = [(gx, gy, (gz + o) % ngz) for o in range(1, ngz)]
    na, nb = ngx * 2, (ngy // 2) * ngz
    core = gy % 2
    ma, mb = gx * 2 + core, (gy // 2) * ngz + gz

    def member_a(o):
        m = (ma + o) % na
        return (m // 2, (gy // 2) * 2 + m % 2, gz)

    def member_b(o):
        m = (mb + o) % nb
        return (gx, (m // ngz) * 2 + core, m % ngz)

    group_a = [member_a(o) for o in range(1, na)]
    group_b = [member_b(o) for o in range(1, nb)]

    here = pl.multiple_of(piece * ROWS, ROWS)
    my_rows = pl.ds(here, ROWS)
    loads = []
    for n, (src, dst) in enumerate(
        [
            (bed_in, bed),
            (vel_in, vel),
            (fric_in.at[my_rows, :], fric),
            (fstep_in.at[my_rows, :], fstep),
            (misfit_in.at[my_rows, :], misfit),
        ]
    ):
        copy = pltpu.make_async_copy(src, dst, load_sem.at[n])
        copy.start()
        loads.append(copy)

    barrier = pltpu.get_barrier_semaphore()
    partners = [x_low, x_high, y_low, y_high] + peers + group_a + group_b
    for partner in partners:
        pl.semaphore_signal(barrier, inc=1, device_id=partner, device_id_type=MESH)

    base = gz * depth
    for copy in loads:
        copy.wait()
    bedf = bed[...]
    vb0 = jnp.zeros(bedf.shape, F32)
    vb1 = jnp.zeros(bedf.shape, F32)
    for k in range(depth):
        at = bedf == base + k
        vb0 = jnp.where(at, vel[0, k], vb0)
        vb1 = jnp.where(at, vel[1, k], vb1)
    vbs[0] = vb0
    vbs[1] = vb1

    pl.semaphore_wait(barrier, len(partners))

    layers = pl.ds(base, depth)

    def moves(part, o):
        rows = pl.ds(pl.multiple_of(part * ROWS, ROWS), ROWS)
        return [
            (visc.at[:, rows, :], V.at[layers]),
            (binv.at[:, :, rows, :], B.at[:, layers]),
            (coup.at[:, rows, :], L.at[layers]),
            (vbs.at[:, rows, :], vbp.at[o]),
        ]

    locals_in = []
    for a, (src, dst) in enumerate(moves(piece, 0)):
        copy = pltpu.make_async_copy(src, dst, loc_sem.at[a])
        copy.start()
        locals_in.append(copy)
    incoming = [[], [], [], []]
    per_peer = [moves(piece_of((gz + o) % ngz), o) for o in range(1, ngz)]
    for a in range(4):
        for o in range(1, ngz):
            src, dst = per_peer[o - 1][a]
            copy = pltpu.make_async_remote_copy(
                src_ref=src, dst_ref=dst,
                send_sem=in_send.at[a, o], recv_sem=in_recv.at[a, o],
                device_id=peers[o - 1], device_id_type=MESH,
            )
            copy.start()
            incoming[a].append(copy)

    row = lax.broadcasted_iota(jnp.int32, (ROWS, LANES), 0)
    lane = lax.broadcasted_iota(jnp.int32, (ROWS, LANES), 1)
    column = jnp.zeros((ROWS, LANES), F32)
    for j in range(LANES // TILE):
        flag = ice[piece, j].astype(F32)
        column = jnp.where(lane // TILE == j, flag, column)
    has_ice = column > 0.5
    kbed = jnp.where(has_ice, bed[my_rows, :].astype(F32), NONE)
    friction = fric[...]
    load = misfit[...] * column

    for field in (Z0, ZA, S0, SA, ZB, SB):
        for c in range(2):
            field[c, 0] = jnp.zeros((ROWS, LANES), F32)
            field[c, NZ + 1] = jnp.zeros((ROWS, LANES), F32)
    for ps in (ps0, ps3):
        ps[...] = jnp.zeros(ps.shape, F32)

    def pack_lane(packed, value, j):
        low, high = packed
        low = jnp.where(lane == j, pltpu.roll(value, j, 1), low)
        high = jnp.where(lane == j, pltpu.roll(value, (j + 1) % LANES, 1), high)
        return low, high

    def pack_rows(xs, value, j):
        xs[0, pl.ds(j, 1), :] = value[0:1, :]
        xs[1, pl.ds(j, 1), :] = value[ROWS - 1 : ROWS, :]

    def send_halo(index, xs, xr, ps, pr):
        copies = []
        for side, (src, dst, device) in enumerate(
            [
                (ps.at[0], pr.at[1], y_low),
                (ps.at[1], pr.at[0], y_high),
                (xs.at[0], xr.at[1], x_low),
                (xs.at[1], xr.at[0], x_high),
            ]
        ):
            copy = pltpu.make_async_remote_copy(
                src_ref=src, dst_ref=dst,
                send_sem=halo_send.at[index, side], recv_sem=halo_recv.at[index, side],
                device_id=device, device_id_type=MESH,
            )
            copy.start()
            copies.append(copy)
        return copies

    def beside(value, xr, xj, left, right, lj):
        east = jnp.where(row == ROWS - 1, xr[1, pl.ds(xj, 1), :], pltpu.roll(value, ROWS - 1, 0))
        west = jnp.where(row == 0, xr[0, pl.ds(xj, 1), :], pltpu.roll(value, 1, 0))
        north = jnp.where(
            lane == LANES - 1, pltpu.roll(right, LANES - 1 - lj, 1), pltpu.roll(value, LANES - 1, 1)
        )
        south = jnp.where(
            lane == 0, pltpu.roll(left, (LANES - lj) % LANES, 1), pltpu.roll(value, 1, 1)
        )
        return east, west, north, south

    locals_in[0].wait()
    for copy in incoming[0]:
        copy.wait_recv()

    def pack_viscosity(k, packed):
        value = V[k]
        pack_rows(xs0, value, k)
        return pack_lane(packed, value, k)

    blank = jnp.zeros((ROWS, LANES), F32)
    packed = blocked_loop(NZ, pack_viscosity, (blank, blank))
    pack_rows(xs0, kbed, NZ)
    low, high = pack_lane(packed, kbed, NZ)
    ps0[0] = low
    ps0[1] = high
    halo0 = send_halo(0, xs0, xr0, ps0, pr0)

    for copy in halo0:
        copy.wait_recv()
    left, right = pr0[0], pr0[1]
    bed_e, bed_w, bed_n, bed_s = beside(kbed, xr0, NZ, left, right, NZ)
    bed_e = jnp.where((row == ROWS - 1) & (spot == total_pieces - 1), NONE, bed_e)
    bed_w = jnp.where((row == 0) & (spot == 0), NONE, bed_w)
    bed_n = jnp.where((lane == LANES - 1) & (gy == ngy - 1), NONE, bed_n)
    bed_s = jnp.where((lane == 0) & (gy == 0), NONE, bed_s)

    def layer_weights(k, carry):
        below_v, below_a = carry
        level = jnp.full((ROWS, LANES), k, jnp.int32).astype(F32)
        value = V[k]
        act = jnp.where(level >= kbed, 1.0, 0.0)
        bedflag = jnp.where(level == kbed, 1.0, 0.0)
        east, west, north, south = beside(value, xr0, k, left, right, k)
        half_act = 0.5 * act
        down = (VERTICAL * (value + below_v)) * (half_act * below_a)
        we = (value + east) * jnp.where(level >= bed_e, half_act, 0.0)
        ww = (value + west) * jnp.where(level >= bed_w, half_act, 0.0)
        wn = (value + north) * jnp.where(level >= bed_n, half_act, 0.0)
        ws = (value + south) * jnp.where(level >= bed_s, half_act, 0.0)
        WU[k] = down
        WE[k] = we
        WW[k] = ww
        WN[k] = wn
        WS[k] = ws
        ew, ns = we + ww, wn + ws
        rest = friction * bedflag + (1.0 - act)
        D0[k] = down + STRETCH * ew + ns + rest
        D1[k] = down + ew + STRETCH * ns + rest
        return value, act

    blocked_loop(NZ, layer_weights, (blank, blank))
    WU[NZ] = blank

    for group, copy in zip(incoming[1:], locals_in[1:]):
        copy.wait()
        for remote in group:
            remote.wait_recv()
    speed0 = vbp[0, 0]
    speed1 = vbp[0, 1]
    for o in range(1, ngz):
        speed0 = speed0 + vbp[o, 0]
        speed1 = speed1 + vbp[o, 1]
    speed0 = jnp.where(has_ice, speed0, 0.0)
    speed1 = jnp.where(has_ice, speed1, 0.0)
    drive = friction * fstep[...]
    push0, push1 = drive * speed0, drive * speed1

    def apply_inverse(k, first, second):
        b0, b1, b2 = B[0, k], B[1, k], B[2, k]
        return b0 * first + b1 * second, b1 * first + b2 * second

    def rise(k, first, second, state, out):
        y0, y1, total = state
        link = L[k]
        t0 = first + link * y0
        t1 = second + link * y1
        y0, y1 = apply_inverse(k, t0, t1)
        out[0, k + 1] = y0
        out[1, k + 1] = y1
        return y0, y1, total + (t0 * y0 + t1 * y1)

    def first_rise(k, state):
        level = jnp.full((ROWS, LANES), k, jnp.int32).astype(F32)
        act = jnp.where(level >= kbed, 1.0, 0.0)
        beneath = jnp.where(level - 1.0 >= kbed, 1.0, 0.0)
        rest = 1.0 - act
        B[0, k] = act * B[0, k] + rest
        B[1, k] = act * B[1, k]
        B[2, k] = act * B[2, k] + rest
        L[k] = L[k] * act * beneath
        at = level == kbed
        first = jnp.where(at, push0, 0.0)
        second = jnp.where(at, push1, 0.0)
        above = WU[k + 1]
        D0[k] = D0[k] + above
        D1[k] = D1[k] + above
        return rise(k, first, second, state, Z0)

    state = blocked_loop(NZ, first_rise, (blank, blank, blank))
    rz0 = state[2]

    def fall(k, g0, g1, field):
        add0, add1 = apply_inverse(k, g0, g1)
        z0 = field[0, k + 1] + add0
        z1 = field[1, k + 1] + add1
        field[0, k + 1] = z0
        field[1, k + 1] = z1
        link = L[k]
        return z0, z1, link * z0, link * z1

    def fall_bare(k, g0, g1, field):
        z0, z1 = apply_inverse(k, g0, g1)
        field[0, k + 1] = z0
        field[1, k + 1] = z1
        link = L[k]
        return z0, z1, link * z0, link * z1

    seed_a0, seed_a1 = load * Z0[0, NZ], load * Z0[1, NZ]

    def fall_first(i, carry):
        k = NZ - 1 - i
        g0, g1, a0, a1, low, high = carry
        z0, z1, g0, g1 = fall(k, g0, g1, Z0)
        y0, y1, a0, a1 = fall_bare(k, a0, a1, ZA)
        packed = (low, high)
        for n, value in enumerate((z0, z1, y0, y1)):
            pack_rows(xs1, value, k + NZ * n)
            packed = pack_lane(packed, value, k + NZ * n)
        return (g0, g1, a0, a1) + packed

    carry = blocked_loop(NZ, fall_first, (blank, blank, seed_a0, seed_a1, blank, blank))
    ps1[0] = carry[4]
    ps1[1] = carry[5]
    halo1 = send_halo(1, xs1, xr1, ps1, pr1)
    raa = seed_a0 * ZA[0, NZ] + seed_a1 * ZA[1, NZ]

    def operate(k, weights, field, xr, xj, left, right, lj):
        up, down, we, ww, wn, ws, d0, d1 = weights
        result = []
        for c in range(2):
            value = field[c, k + 1]
            east, west, north, south = beside(
                value, xr, xj + c * NZ + k, left, right, lj + c * NZ + k
            )
            vertical = up * field[c, k + 2] + down * field[c, k]
            ew = we * east + ww * west
            ns = wn * north + ws * south
            if c == 0:
                result.append(d0 * value - vertical - STRETCH * ew - ns)
            else:
                result.append(d1 * value - vertical - ew - STRETCH * ns)
        return result

    def weights_of(k):
        return WU[k + 1], WU[k], WE[k], WW[k], WN[k], WS[k], D0[k], D1[k]

    def against(field, k, image, total):
        return total + (field[0, k + 1] * image[0] + field[1, k + 1] * image[1])

    for copy in halo1:
        copy.wait_recv()
    left1, right1 = pr1[0], pr1[1]

    def middle_rise(k, carry):
        pq0, paa, main, extra = carry
        weights = weights_of(k)
        w = operate(k, weights, Z0, xr1, 0, left1, right1, 0)
        wa = operate(k, weights, ZA, xr1, 2 * NZ, left1, right1, 2 * NZ)
        pq0 = against(Z0, k, w, pq0)
        paa = against(ZA, k, wa, paa)
        main = rise(k, w[0], w[1], main, S0)
        extra = rise(k, wa[0], wa[1], extra, SA)
        return pq0, paa, main, extra

    triple = (blank, blank, blank)
    pq0, paa, main, extra = blocked_loop(NZ, middle_rise, (blank, blank, triple, triple))
    g0, gaa = main[2], extra[2]
    seed_b0, seed_b1 = load * S0[0, NZ], load * S0[1, NZ]

    def fall_second(i, carry):
        k = NZ - 1 - i
        g0, g1, h0, h1, b0, b1, low1, high1, low2, high2 = carry
        z0, z1, g0, g1 = fall(k, g0, g1, S0)
        a0, a1, h0, h1 = fall(k, h0, h1, SA)
        y0, y1, b0, b1 = fall_bare(k, b0, b1, ZB)
        packed = (low1, high1)
        for n, value in enumerate((y0, y1, z0, z1)):
            pack_rows(xs2, value, k + NZ * n)
            packed = pack_lane(packed, value, k + NZ * n)
        other = (low2, high2)
        for n, value in enumerate((a0, a1)):
            pack_rows(xs2, value, k + NZ * (n + 4))
            other = pack_lane(other, value, k + NZ * n)
        return (g0, g1, h0, h1, b0, b1) + packed + other

    carry = blocked_loop(
        NZ, fall_second, (blank, blank, blank, blank, seed_b0, seed_b1, blank, blank, blank, blank)
    )
    for n in range(2):
        ps2[0, ROWS * n : ROWS * (n + 1), :] = carry[6 + 2 * n]
        ps2[1, ROWS * n : ROWS * (n + 1), :] = carry[7 + 2 * n]
    halo2 = send_halo(2, xs2, xr2, ps2, pr2)
    rab = seed_a0 * ZB[0, NZ] + seed_a1 * ZB[1, NZ]
    rbb = seed_b0 * ZB[0, NZ] + seed_b1 * ZB[1, NZ]

    for copy in halo2:
        copy.wait_recv()
    left2, right2 = pr2[0, :ROWS, :], pr2[1, :ROWS, :]
    left3, right3 = pr2[0, ROWS:, :], pr2[1, ROWS:, :]

    def last_rise(k, carry):
        pab, pbb, gab, main = carry
        w = operate(k, weights_of(k), ZB, xr2, 0, left2, right2, 0)
        pab = against(ZA, k, w, pab)
        pbb = against(ZB, k, w, pbb)
        gab = against(SA, k, w, gab)
        main = rise(k, w[0], w[1], main, SB)
        return pab, pbb, gab, main

    pab, pbb, gab, main = blocked_loop(NZ, last_rise, (blank, blank, blank, triple))
    gbb = main[2]

    def fall_third(i, carry):
        k = NZ - 1 - i
        g0, g1, low, high = carry
        z0, z1, g0, g1 = fall(k, g0, g1, SB)
        packed = (low, high)
        for n, value in enumerate((z0, z1)):
            pack_rows(xs3, value, k + NZ * n)
            packed = pack_lane(packed, value, k + NZ * n)
        return (g0, g1) + packed

    carry = blocked_loop(NZ, fall_third, (blank, blank, blank, blank))
    ps3[0] = carry[2]
    ps3[1] = carry[3]
    halo3 = send_halo(3, xs3, xr3, ps3, pr3)

    def early_energy(k, carry):
        d0, daa = carry
        weights = weights_of(k)
        w = operate(k, weights, S0, xr2, 2 * NZ, left2, right2, 2 * NZ)
        wa = operate(k, weights, SA, xr2, 4 * NZ, left3, right3, 0)
        return against(S0, k, w, d0), against(SA, k, wa, daa)

    d0, daa = blocked_loop(NZ, early_energy, (blank, blank))

    stages = ((group_a, ra, red_recv_a), (group_b, rb, red_recv_b))

    def gather_sums(values, turn):
        for n, value in enumerate(values):
            stack[turn, n : n + 1, :] = jnp.sum(value, axis=0, keepdims=True)
        each = jnp.sum(stack[turn], axis=1, keepdims=True)
        return jnp.sum(jnp.where(lane == row, each, 0.0), axis=0, keepdims=True)

    def send_sum(turn, stage, value):
        rt[turn, stage] = value
        group, received, sem = stages[stage]
        copies = []
        for o, device in enumerate(group):
            copy = pltpu.make_async_remote_copy(
                src_ref=rt.at[turn, stage], dst_ref=received.at[turn, o],
                send_sem=red_send.at[turn, stage, o], recv_sem=sem.at[turn, o],
                device_id=device, device_id_type=MESH,
            )
            copy.start()
            copies.append(copy)
        return copies

    def finish_sum(turn, stage, copies):
        for copy in copies:
            copy.wait_recv()
        received = stages[stage][1]
        return rt[turn, stage] + jnp.sum(received[turn], axis=0)

    def spread(total, count):
        each = jnp.sum(jnp.where(lane == row, total, 0.0), axis=1, keepdims=True)
        each = jnp.broadcast_to(each, (ROWS, LANES))
        return [each[n : n + 1, :] for n in range(count)]

    stack[...] = jnp.zeros(stack.shape, F32)
    first_a = send_sum(0, 0, gather_sums([rz0, pq0, g0, d0], 0))

    for copy in halo3:
        copy.wait_recv()
    left4, right4 = pr3[0], pr3[1]

    def late_energy(k, carry):
        dab, dbb = carry
        w = operate(k, weights_of(k), SB, xr3, 0, left4, right4, 0)
        return against(SA, k, w, dab), against(SB, k, w, dbb)

    dab, dbb = blocked_loop(NZ, late_energy, (blank, blank))

    second_a = send_sum(
        1, 0, gather_sums([raa, rab, rbb, paa, pab, pbb, gaa, gab, gbb, daa, dab, dbb], 1)
    )
    first_b = send_sum(0, 1, finish_sum(0, 0, first_a))
    second_b = send_sum(1, 1, finish_sum(1, 0, second_a))
    reductions = first_a + second_a + first_b + second_b
    rz0, pq0, g0, d0 = spread(finish_sum(0, 1, first_b), 4)

    def combination(rz, pq, g, d):
        step = rz / pq
        renewed = step * step * g - rz
        grow = 1.0 + renewed / rz
        energy = grow * grow * pq - 2.0 * grow * step * g + step * step * d
        second = renewed / energy
        return step + second * grow, -(second * step)

    c0, c1 = combination(rz0, pq0, g0, d0)

    def increments(k, carry):
        for c in range(2):
            Z0[c, k + 1] = c0 * Z0[c, k + 1] + c1 * S0[c, k + 1]
        return carry

    blocked_loop(NZ, increments, 0)
    finals = []
    rest = []
    back = (inc.at[:, :, my_rows, :], adj.at[:, :, my_rows, :], hess.at[my_rows, :])

    def give_back(n, field):
        copy = pltpu.make_async_copy(field.at[:, pl.ds(1 + base, depth)], back[n], loc_sem.at[n])
        copy.start()
        finals.append(copy)
        for o in range(1, ngz):
            theirs = pl.ds(1 + ((gz + o) % ngz) * depth, depth)
            send_back(n, o, field.at[:, theirs])

    def send_back(n, o, src):
        copy = pltpu.make_async_remote_copy(
            src_ref=src, dst_ref=back[n],
            send_sem=out_send.at[n, o], recv_sem=out_recv.at[n, o],
            device_id=peers[o - 1], device_id_type=MESH,
        )
        copy.start()
        rest.append(copy)

    give_back(0, Z0)

    raa, rab, rbb, paa, pab, pbb, gaa, gab, gbb, daa, dab, dbb = spread(finish_sum(1, 1, second_b), 12)

    def form(aa, ab, bb):
        return c0 * c0 * aa + 2.0 * (c0 * c1) * ab + c1 * c1 * bb

    e0, e1 = combination(form(raa, rab, rbb), form(paa, pab, pbb), form(gaa, gab, gbb), form(daa, dab, dbb))
    f_za, f_zb, f_sa, f_sb = e0 * c0, e0 * c1, e1 * c0, e1 * c1

    def adjoints(k, carry):
        level = jnp.full((ROWS, LANES), k, jnp.int32).astype(F32)
        at = level == kbed
        out = []
        for c in range(2):
            value = (f_za * ZA[c, k + 1] + f_zb * ZB[c, k + 1]) + (f_sa * SA[c, k + 1] + f_sb * SB[c, k + 1])
            ZA[c, k + 1] = value
            out.append(jnp.where(at, value, carry[c]))
        return tuple(out)

    basal = blocked_loop(NZ, adjoints, (blank, blank))
    give_back(1, ZA)
    action = friction * (speed0 * basal[0] + speed1 * basal[1])
    hess[my_rows, :] = action
    vbs[0, my_rows, :] = action
    for o in range(1, ngz):
        send_back(2, o, vbs.at[0, my_rows, :])
    for copy in finals:
        copy.wait()
    for copy in rest:
        copy.wait()
    for group in incoming:
        for copy in group:
            copy.wait_send()
    for copy in halo0 + halo1 + halo2 + halo3 + reductions:
        copy.wait_send()


def local(sizes, *args):
    ngx, ngy, ngz = sizes
    field = pltpu.VMEM((NZ, ROWS, LANES), F32)
    state = pltpu.VMEM((2, NZ + 2, ROWS, LANES), F32)
    depth, rows, lanes = args[1].shape
    dma = pltpu.SemaphoreType.DMA

    def halo(length, packs):
        return [pltpu.VMEM((2, length, LANES), F32)] * 2 + [pltpu.VMEM((2, packs * ROWS, LANES), F32)] * 2

    na, nb = ngx * 2, (ngy // 2) * ngz
    scratch = (
        [pltpu.VMEM((2, depth, rows, lanes), F32), pltpu.VMEM((rows, lanes), jnp.int32)]
        + [pltpu.VMEM((ROWS, LANES), F32)] * 3
        + [field, pltpu.VMEM((3, NZ, ROWS, LANES), F32), field]
        + [pltpu.VMEM((2, rows, lanes), F32), pltpu.VMEM((ngz, 2, ROWS, LANES), F32)]
        + [pltpu.VMEM((NZ + 1, ROWS, LANES), F32)]
        + [field] * 6
        + [state] * 6
        + halo(NZ + 8, 1) + halo(4 * NZ, 1) + halo(6 * NZ, 2) + halo(2 * NZ, 1)
        + [pltpu.VMEM((2, ROWS, LANES), F32), pltpu.VMEM((2, 2, 1, LANES), F32)]
        + [pltpu.VMEM((2, na - 1, 1, LANES), F32), pltpu.VMEM((2, nb - 1, 1, LANES), F32)]
        + [dma((5,)), dma((4,)), dma((4, ngz)), dma((4, ngz)), dma((4, 4)), dma((4, 4))]
        + [dma((2, 2, max(na, nb))), dma((2, na)), dma((2, nb)), dma((3, ngz)), dma((3, ngz))]
    )
    vmem = pl.BlockSpec(memory_space=pltpu.VMEM)
    hbm = pl.BlockSpec(memory_space=pl.ANY)
    smem = pl.BlockSpec(memory_space=pltpu.SMEM)
    return pl.pallas_call(
        functools.partial(kernel, sizes),
        out_shape=(
            jax.ShapeDtypeStruct((2, depth, rows, lanes), F32),
            jax.ShapeDtypeStruct((2, depth, rows, lanes), F32),
            jax.ShapeDtypeStruct((rows, lanes), F32),
        ),
        in_specs=[hbm] * 7 + [smem, hbm],
        out_specs=(hbm, hbm, vmem),
        scratch_shapes=scratch,
        compiler_params=pltpu.CompilerParams(
            collective_id=0, has_side_effects=True, vmem_limit_bytes=62 * 1024 * 1024
        ),
    )(*args)


def solution(mesh):
    sizes = (mesh.shape["gx"], mesh.shape["gy"], mesh.shape["gz"])
    wide, cell, flat = P(None, "gz", "gx", "gy"), P("gz", "gx", "gy"), P("gx", "gy")
    return jax.shard_map(
        functools.partial(local, sizes),
        mesh=mesh,
        in_specs=(wide, cell, wide, cell, flat, flat, flat, flat, flat),
        out_specs=(wide, wide, flat),
        check_vma=False,
    )
```

```python
import functools

import jax
import jax.numpy as jnp
from jax import lax
from jax.experimental import pallas as pl
from jax.experimental.pallas import tpu as pltpu
from jax.sharding import PartitionSpec as P

TILE = 16
VERTICAL = 8.0
STRETCH = 4.0
NONE = 1000.0
MESH = pl.DeviceIdType.MESH
F32 = jnp.float32
NZ = 32
ROWS = 16
LANES = 128
UNROLL = 32


def blocked_loop(steps, body, carry):
    def chunk(index, state):
        for inner in range(UNROLL):
            state = body(index * UNROLL + inner, state)
        return state

    return lax.fori_loop(0, steps // UNROLL, chunk, carry)


def kernel(
    sizes,
    vel_in, visc, binv, coup, fric_in, fstep_in, misfit_in, ice, bed_in,
    inc, adj, hess,
    vel, bed, fric, fstep, misfit,
    V, B, L, vbs, vbp, WU, WE, WW, WN, WS, D0, D1,
    Z0, ZA, S0, SA, ZB, SB,
    xs0, xr0, ps0, pr0, xs1, xr1, ps1, pr1, xs2, xr2, ps2, pr2, xs3, xr3, ps3, pr3,
    stack, rt, ra, rb,
    load_sem, loc_sem, in_send, in_recv, halo_send, halo_recv, red_send, red_recv_a, red_recv_b,
    out_send, out_recv,
):
    ngx, ngy, ngz = sizes
    gx, gy, gz = lax.axis_index("gx"), lax.axis_index("gy"), lax.axis_index("gz")
    depth = NZ // ngz
    odd = lax.rem(gx, 2)

    def around(index, count):
        return [index] + [lax.rem(index + o, count) for o in range(1, count)]

    def piece_of(q):
        return q + odd * (ngz - 1 - 2 * q)

    gxs, gzs = around(gx, ngx), around(gz, ngz)
    pieces = [piece_of(q) for q in gzs]
    piece = pieces[0]
    total_pieces = ngx * ngz
    spot = gx * ngz + piece

    def holder(index):
        block = lax.div(index, ngz)
        part = index - block * ngz
        return (block, gy, part + lax.rem(block, 2) * (ngz - 1 - 2 * part))

    x_low = holder(lax.rem(spot + (total_pieces - 1), total_pieces))
    x_high = holder(lax.rem(spot + 1, total_pieces))
    y_low = (gx, lax.rem(gy + (ngy - 1), ngy), gz)
    y_high = (gx, lax.rem(gy + 1, ngy), gz)
    peers = [(gx, gy, q) for q in gzs[1:]]
    chips = ngy // 2
    na, nb = ngx * 2, chips * ngz
    chip = lax.div(gy, 2)
    core = gy - 2 * chip
    same_core = [2 * c + core for c in around(chip, chips)]
    other_core = 2 * chip + 1 - core
    ma, mb = gx * 2 + core, chip * ngz + gz
    y_other = (gx, lax.rem(gy + ngy + 2 * core - 1, ngy), gz)

    def ring(offset, count):
        return min(offset, count - offset)

    steps_a = sorted(
        ((i, j) for i in range(ngx) for j in range(2) if i or j), key=lambda step: -ring(step[0], ngx)
    )
    steps_b = sorted(
        ((i, j) for i in range(chips) for j in range(ngz) if i or j),
        key=lambda step: -ring(step[0], chips) - ring(step[1], ngz),
    )
    group_a = [(gxs[i], other_core if j else gy, gz) for i, j in steps_a]
    group_b = [(gx, same_core[i], gzs[j]) for i, j in steps_b]

    here = pl.multiple_of(piece * ROWS, ROWS)
    my_rows = pl.ds(here, ROWS)
    loads = []
    for n, (src, dst) in enumerate(
        [
            (bed_in, bed),
            (vel_in, vel),
            (fric_in.at[my_rows, :], fric),
            (fstep_in.at[my_rows, :], fstep),
            (misfit_in.at[my_rows, :], misfit),
        ]
    ):
        copy = pltpu.make_async_copy(src, dst, load_sem.at[n])
        copy.start()
        loads.append(copy)

    barrier = pltpu.get_barrier_semaphore()
    far = [(-ring(i, ngx), device) for (i, _), device in zip(steps_a, group_a)]
    far += [(-ring(i, chips) - ring(j, ngz), device) for (i, j), device in zip(steps_b, group_b)]
    partners = [device for _, device in sorted(far, key=lambda item: item[0])] + [y_other]
    for partner in partners:
        pl.semaphore_signal(barrier, inc=1, device_id=partner, device_id_type=MESH)

    base = gz * depth
    for copy in loads:
        copy.wait()
    bedf = bed[...]
    vb0 = jnp.zeros(bedf.shape, F32)
    vb1 = jnp.zeros(bedf.shape, F32)
    for k in range(depth):
        at = bedf == base + k
        vb0 = jnp.where(at, vel[0, k], vb0)
        vb1 = jnp.where(at, vel[1, k], vb1)
    vbs[0] = vb0
    vbs[1] = vb1

    pl.semaphore_wait(barrier, len(partners))

    layers = pl.ds(base, depth)

    def moves(part, o):
        rows = pl.ds(pl.multiple_of(part * ROWS, ROWS), ROWS)
        return [
            (visc.at[:, rows, :], V.at[layers]),
            (binv.at[:, :, rows, :], B.at[:, layers]),
            (coup.at[:, rows, :], L.at[layers]),
            (vbs.at[:, rows, :], vbp.at[o]),
        ]

    locals_in = []
    for a, (src, dst) in enumerate(moves(piece, 0)):
        copy = pltpu.make_async_copy(src, dst, loc_sem.at[a])
        copy.start()
        locals_in.append(copy)
    incoming = [[], [], [], []]
    per_peer = [moves(pieces[o], o) for o in range(1, ngz)]
    for a in range(4):
        for o in range(1, ngz):
            src, dst = per_peer[o - 1][a]
            copy = pltpu.make_async_remote_copy(
                src_ref=src, dst_ref=dst,
                send_sem=in_send.at[a, o], recv_sem=in_recv.at[a, o],
                device_id=peers[o - 1], device_id_type=MESH,
            )
            copy.start()
            incoming[a].append(copy)

    row = lax.broadcasted_iota(jnp.int32, (ROWS, LANES), 0)
    lane = lax.broadcasted_iota(jnp.int32, (ROWS, LANES), 1)
    column = jnp.zeros((ROWS, LANES), F32)
    for j in range(LANES // TILE):
        flag = ice[piece, j].astype(F32)
        column = jnp.where(lane // TILE == j, flag, column)
    has_ice = column > 0.5
    kbed = jnp.where(has_ice, bed[my_rows, :].astype(F32), NONE)
    friction = fric[...]
    load = misfit[...] * column

    for field in (Z0, ZA, S0, SA, ZB, SB):
        for c in range(2):
            field[c, 0] = jnp.zeros((ROWS, LANES), F32)
            field[c, NZ + 1] = jnp.zeros((ROWS, LANES), F32)
    V[NZ] = jnp.zeros((ROWS, LANES), F32)
    for ps in (ps0, ps3):
        ps[...] = jnp.zeros(ps.shape, F32)

    def pack_lane(packed, value, j):
        low, high = packed
        low = jnp.where(lane == j, pltpu.roll(value, j, 1), low)
        high = jnp.where(lane == j, pltpu.roll(value, (j + 1) % LANES, 1), high)
        return low, high

    def pack_rows(xs, value, j):
        xs[0, pl.ds(j, 1), :] = value[0:1, :]
        xs[1, pl.ds(j, 1), :] = value[ROWS - 1 : ROWS, :]

    def send_halo(index, xs, xr, ps, pr):
        copies = []
        for side, (src, dst, device) in enumerate(
            [
                (ps.at[0], pr.at[1], y_low),
                (ps.at[1], pr.at[0], y_high),
                (xs.at[0], xr.at[1], x_low),
                (xs.at[1], xr.at[0], x_high),
            ]
        ):
            copy = pltpu.make_async_remote_copy(
                src_ref=src, dst_ref=dst,
                send_sem=halo_send.at[index, side], recv_sem=halo_recv.at[index, side],
                device_id=device, device_id_type=MESH,
            )
            copy.start()
            copies.append(copy)
        return copies

    def beside(value, xr, xj, left, right, lj):
        east = jnp.where(row == ROWS - 1, xr[1, pl.ds(xj, 1), :], pltpu.roll(value, ROWS - 1, 0))
        west = jnp.where(row == 0, xr[0, pl.ds(xj, 1), :], pltpu.roll(value, 1, 0))
        north = jnp.where(
            lane == LANES - 1, pltpu.roll(right, LANES - 1 - lj, 1), pltpu.roll(value, LANES - 1, 1)
        )
        south = jnp.where(
            lane == 0, pltpu.roll(left, (LANES - lj) % LANES, 1), pltpu.roll(value, 1, 1)
        )
        return east, west, north, south

    locals_in[0].wait()
    for copy in incoming[0]:
        copy.wait_recv()

    def pack_viscosity(k, packed):
        value = V[k]
        pack_rows(xs0, value, k)
        return pack_lane(packed, value, k)

    blank = jnp.zeros((ROWS, LANES), F32)
    packed = blocked_loop(NZ, pack_viscosity, (blank, blank))
    pack_rows(xs0, kbed, NZ)
    low, high = pack_lane(packed, kbed, NZ)
    ps0[0] = low
    ps0[1] = high
    halo0 = send_halo(0, xs0, xr0, ps0, pr0)

    for group, copy in zip(incoming[1:], locals_in[1:]):
        copy.wait()
        for remote in group:
            remote.wait_recv()
    speed0 = vbp[0, 0]
    speed1 = vbp[0, 1]
    for o in range(1, ngz):
        speed0 = speed0 + vbp[o, 0]
        speed1 = speed1 + vbp[o, 1]
    speed0 = jnp.where(has_ice, speed0, 0.0)
    speed1 = jnp.where(has_ice, speed1, 0.0)
    drive = friction * fstep[...]
    push0, push1 = drive * speed0, drive * speed1

    def apply_inverse(k, first, second):
        b0, b1, b2 = B[0, k], B[1, k], B[2, k]
        return b0 * first + b1 * second, b1 * first + b2 * second

    def rise(k, first, second, state, out):
        y0, y1, total = state
        link = L[k]
        t0 = first + link * y0
        t1 = second + link * y1
        y0, y1 = apply_inverse(k, t0, t1)
        out[0, k + 1] = y0
        out[1, k + 1] = y1
        return y0, y1, total + (t0 * y0 + t1 * y1)

    def first_rise(k, state):
        level = jnp.full((ROWS, LANES), k, jnp.int32).astype(F32)
        act = jnp.where(level >= kbed, 1.0, 0.0)
        beneath = jnp.where(level - 1.0 >= kbed, 1.0, 0.0)
        rest = 1.0 - act
        B[0, k] = act * B[0, k] + rest
        B[1, k] = act * B[1, k]
        B[2, k] = act * B[2, k] + rest
        L[k] = L[k] * act * beneath
        at = level == kbed
        first = jnp.where(at, push0, 0.0)
        second = jnp.where(at, push1, 0.0)
        return rise(k, first, second, state, Z0)

    state = blocked_loop(NZ, first_rise, (blank, blank, blank))
    rz0 = state[2]

    def fall(k, g0, g1, field):
        add0, add1 = apply_inverse(k, g0, g1)
        z0 = field[0, k + 1] + add0
        z1 = field[1, k + 1] + add1
        field[0, k + 1] = z0
        field[1, k + 1] = z1
        link = L[k]
        return z0, z1, link * z0, link * z1

    def fall_bare(k, g0, g1, field):
        z0, z1 = apply_inverse(k, g0, g1)
        field[0, k + 1] = z0
        field[1, k + 1] = z1
        link = L[k]
        return z0, z1, link * z0, link * z1

    seed_a0, seed_a1 = load * Z0[0, NZ], load * Z0[1, NZ]

    def fall_first(i, carry):
        k = NZ - 1 - i
        g0, g1, a0, a1, low, high = carry
        z0, z1, g0, g1 = fall(k, g0, g1, Z0)
        y0, y1, a0, a1 = fall_bare(k, a0, a1, ZA)
        packed = (low, high)
        for n, value in enumerate((z0, z1, y0, y1)):
            pack_rows(xs1, value, k + NZ * n)
            packed = pack_lane(packed, value, k + NZ * n)
        return (g0, g1, a0, a1) + packed

    carry = blocked_loop(NZ, fall_first, (blank, blank, seed_a0, seed_a1, blank, blank))
    ps1[0] = carry[4]
    ps1[1] = carry[5]
    halo1 = send_halo(1, xs1, xr1, ps1, pr1)
    raa = seed_a0 * ZA[0, NZ] + seed_a1 * ZA[1, NZ]

    for copy in halo0:
        copy.wait_recv()
    left, right = pr0[0], pr0[1]
    bed_e, bed_w, bed_n, bed_s = beside(kbed, xr0, NZ, left, right, NZ)
    bed_e = jnp.where((row == ROWS - 1) & (spot == total_pieces - 1), NONE, bed_e)
    bed_w = jnp.where((row == 0) & (spot == 0), NONE, bed_w)
    bed_n = jnp.where((lane == LANES - 1) & (gy == ngy - 1), NONE, bed_n)
    bed_s = jnp.where((lane == 0) & (gy == 0), NONE, bed_s)

    def layer_weights(k, down):
        level = jnp.full((ROWS, LANES), k, jnp.int32).astype(F32)
        value = V[k]
        act = jnp.where(level >= kbed, 1.0, 0.0)
        above = jnp.where((level + 1.0 >= kbed) & (level + 1.0 < NZ), 1.0, 0.0)
        bedflag = jnp.where(level == kbed, 1.0, 0.0)
        east, west, north, south = beside(value, xr0, k, left, right, k)
        half_act = 0.5 * act
        up = (VERTICAL * (value + V[k + 1])) * (half_act * above)
        we = (value + east) * jnp.where(level >= bed_e, half_act, 0.0)
        ww = (value + west) * jnp.where(level >= bed_w, half_act, 0.0)
        wn = (value + north) * jnp.where(level >= bed_n, half_act, 0.0)
        ws = (value + south) * jnp.where(level >= bed_s, half_act, 0.0)
        WU[k + 1] = up
        WE[k] = we
        WW[k] = ww
        WN[k] = wn
        WS[k] = ws
        ew, ns = we + ww, wn + ws
        rest = (up + down) + friction * bedflag + (1.0 - act)
        D0[k] = STRETCH * ew + ns + rest
        D1[k] = ew + STRETCH * ns + rest
        return up

    WU[0] = blank
    blocked_loop(NZ, layer_weights, blank)

    def operate(k, weights, field, xr, xj, left, right, lj):
        up, down, we, ww, wn, ws, d0, d1 = weights
        result = []
        for c in range(2):
            value = field[c, k + 1]
            east, west, north, south = beside(
                value, xr, xj + c * NZ + k, left, right, lj + c * NZ + k
            )
            vertical = up * field[c, k + 2] + down * field[c, k]
            ew = we * east + ww * west
            ns = wn * north + ws * south
            if c == 0:
                result.append(d0 * value - vertical - STRETCH * ew - ns)
            else:
                result.append(d1 * value - vertical - ew - STRETCH * ns)
        return result

    def weights_of(k):
        return WU[k + 1], WU[k], WE[k], WW[k], WN[k], WS[k], D0[k], D1[k]

    def against(field, k, image, total):
        return total + (field[0, k + 1] * image[0] + field[1, k + 1] * image[1])

    for copy in halo1:
        copy.wait_recv()
    left1, right1 = pr1[0], pr1[1]

    def middle_rise(k, carry):
        pq0, paa, main, extra = carry
        weights = weights_of(k)
        w = operate(k, weights, Z0, xr1, 0, left1, right1, 0)
        wa = operate(k, weights, ZA, xr1, 2 * NZ, left1, right1, 2 * NZ)
        pq0 = against(Z0, k, w, pq0)
        paa = against(ZA, k, wa, paa)
        main = rise(k, w[0], w[1], main, S0)
        extra = rise(k, wa[0], wa[1], extra, SA)
        return pq0, paa, main, extra

    triple = (blank, blank, blank)
    pq0, paa, main, extra = blocked_loop(NZ, middle_rise, (blank, blank, triple, triple))
    g0, gaa = main[2], extra[2]
    seed_b0, seed_b1 = load * S0[0, NZ], load * S0[1, NZ]

    def fall_second(i, carry):
        k = NZ - 1 - i
        g0, g1, h0, h1, b0, b1, low1, high1, low2, high2 = carry
        z0, z1, g0, g1 = fall(k, g0, g1, S0)
        a0, a1, h0, h1 = fall(k, h0, h1, SA)
        y0, y1, b0, b1 = fall_bare(k, b0, b1, ZB)
        packed = (low1, high1)
        for n, value in enumerate((y0, y1, z0, z1)):
            pack_rows(xs2, value, k + NZ * n)
            packed = pack_lane(packed, value, k + NZ * n)
        other = (low2, high2)
        for n, value in enumerate((a0, a1)):
            pack_rows(xs2, value, k + NZ * (n + 4))
            other = pack_lane(other, value, k + NZ * n)
        return (g0, g1, h0, h1, b0, b1) + packed + other

    carry = blocked_loop(
        NZ, fall_second, (blank, blank, blank, blank, seed_b0, seed_b1, blank, blank, blank, blank)
    )
    for n in range(2):
        ps2[0, ROWS * n : ROWS * (n + 1), :] = carry[6 + 2 * n]
        ps2[1, ROWS * n : ROWS * (n + 1), :] = carry[7 + 2 * n]
    halo2 = send_halo(2, xs2, xr2, ps2, pr2)
    rab = seed_a0 * ZB[0, NZ] + seed_a1 * ZB[1, NZ]
    rbb = seed_b0 * ZB[0, NZ] + seed_b1 * ZB[1, NZ]

    for copy in halo2:
        copy.wait_recv()
    left2, right2 = pr2[0, :ROWS, :], pr2[1, :ROWS, :]
    left3, right3 = pr2[0, ROWS:, :], pr2[1, ROWS:, :]

    def last_rise(k, carry):
        pab, pbb, gab, main = carry
        w = operate(k, weights_of(k), ZB, xr2, 0, left2, right2, 0)
        pab = against(ZA, k, w, pab)
        pbb = against(ZB, k, w, pbb)
        gab = against(SA, k, w, gab)
        main = rise(k, w[0], w[1], main, SB)
        return pab, pbb, gab, main

    pab, pbb, gab, main = blocked_loop(NZ, last_rise, (blank, blank, blank, triple))
    gbb = main[2]

    def fall_third(i, carry):
        k = NZ - 1 - i
        g0, g1, low, high = carry
        z0, z1, g0, g1 = fall(k, g0, g1, SB)
        packed = (low, high)
        for n, value in enumerate((z0, z1)):
            pack_rows(xs3, value, k + NZ * n)
            packed = pack_lane(packed, value, k + NZ * n)
        return (g0, g1) + packed

    carry = blocked_loop(NZ, fall_third, (blank, blank, blank, blank))
    ps3[0] = carry[2]
    ps3[1] = carry[3]
    halo3 = send_halo(3, xs3, xr3, ps3, pr3)

    def early_energy(k, carry):
        d0, daa = carry
        weights = weights_of(k)
        w = operate(k, weights, S0, xr2, 2 * NZ, left2, right2, 2 * NZ)
        wa = operate(k, weights, SA, xr2, 4 * NZ, left3, right3, 0)
        return against(S0, k, w, d0), against(SA, k, wa, daa)

    d0, daa = blocked_loop(NZ, early_energy, (blank, blank))

    stages = ((group_a, ra, red_recv_a, ma), (group_b, rb, red_recv_b, mb))

    def gather_sums(values, turn):
        for n, value in enumerate(values):
            stack[turn, n : n + 1, :] = jnp.sum(value, axis=0, keepdims=True)
        each = jnp.sum(stack[turn], axis=1, keepdims=True)
        return jnp.sum(jnp.where(lane == row, each, 0.0), axis=0, keepdims=True)

    def send_sum(turn, stage, value):
        rt[turn, stage] = value
        group, received, sem, place = stages[stage]
        received[turn, place] = value
        copies = []
        for o, device in enumerate(group):
            copy = pltpu.make_async_remote_copy(
                src_ref=rt.at[turn, stage], dst_ref=received.at[turn, place],
                send_sem=red_send.at[turn, stage, o], recv_sem=sem.at[turn, o],
                device_id=device, device_id_type=MESH,
            )
            copy.start()
            copies.append(copy)
        return copies

    def finish_sum(turn, stage, copies):
        for copy in copies:
            copy.wait_recv()
        received = stages[stage][1]
        return jnp.sum(received[turn], axis=0)

    def spread(total, count):
        each = jnp.sum(jnp.where(lane == row, total, 0.0), axis=1, keepdims=True)
        each = jnp.broadcast_to(each, (ROWS, LANES))
        return [each[n : n + 1, :] for n in range(count)]

    stack[...] = jnp.zeros(stack.shape, F32)
    first_a = send_sum(0, 0, gather_sums([rz0, pq0, g0, d0], 0))

    for copy in halo3:
        copy.wait_recv()
    left4, right4 = pr3[0], pr3[1]

    def late_energy(k, carry):
        dab, dbb = carry
        w = operate(k, weights_of(k), SB, xr3, 0, left4, right4, 0)
        return against(SA, k, w, dab), against(SB, k, w, dbb)

    dab, dbb = blocked_loop(NZ, late_energy, (blank, blank))

    second_a = send_sum(
        1, 0, gather_sums([raa, rab, rbb, paa, pab, pbb, gaa, gab, gbb, daa, dab, dbb], 1)
    )
    first_b = send_sum(0, 1, finish_sum(0, 0, first_a))
    second_b = send_sum(1, 1, finish_sum(1, 0, second_a))
    reductions = first_a + second_a + first_b + second_b
    rz0, pq0, g0, d0 = spread(finish_sum(0, 1, first_b), 4)

    def combination(rz, pq, g, d):
        step = rz / pq
        renewed = step * step * g - rz
        grow = 1.0 + renewed / rz
        energy = grow * grow * pq - 2.0 * grow * step * g + step * step * d
        second = renewed / energy
        return step + second * grow, -(second * step)

    c0, c1 = combination(rz0, pq0, g0, d0)

    def increments(k, carry):
        for c in range(2):
            Z0[c, k + 1] = c0 * Z0[c, k + 1] + c1 * S0[c, k + 1]
        return carry

    blocked_loop(NZ, increments, 0)
    finals = []
    rest = []
    back = (inc.at[:, :, my_rows, :], adj.at[:, :, my_rows, :], hess.at[my_rows, :])

    def give_back(n, field):
        copy = pltpu.make_async_copy(field.at[:, pl.ds(1 + base, depth)], back[n], loc_sem.at[n])
        copy.start()
        finals.append(copy)
        for o in range(1, ngz):
            theirs = pl.ds(1 + gzs[o] * depth, depth)
            send_back(n, o, field.at[:, theirs])

    def send_back(n, o, src):
        copy = pltpu.make_async_remote_copy(
            src_ref=src, dst_ref=back[n],
            send_sem=out_send.at[n, o], recv_sem=out_recv.at[n, o],
            device_id=peers[o - 1], device_id_type=MESH,
        )
        copy.start()
        rest.append(copy)

    give_back(0, Z0)

    raa, rab, rbb, paa, pab, pbb, gaa, gab, gbb, daa, dab, dbb = spread(finish_sum(1, 1, second_b), 12)

    def form(aa, ab, bb):
        return c0 * c0 * aa + 2.0 * (c0 * c1) * ab + c1 * c1 * bb

    e0, e1 = combination(form(raa, rab, rbb), form(paa, pab, pbb), form(gaa, gab, gbb), form(daa, dab, dbb))
    f_za, f_zb, f_sa, f_sb = e0 * c0, e0 * c1, e1 * c0, e1 * c1

    def adjoints(k, carry):
        level = jnp.full((ROWS, LANES), k, jnp.int32).astype(F32)
        at = level == kbed
        out = []
        for c in range(2):
            value = (f_za * ZA[c, k + 1] + f_zb * ZB[c, k + 1]) + (f_sa * SA[c, k + 1] + f_sb * SB[c, k + 1])
            ZA[c, k + 1] = value
            out.append(jnp.where(at, value, carry[c]))
        return tuple(out)

    basal = blocked_loop(NZ, adjoints, (blank, blank))
    give_back(1, ZA)
    action = friction * (speed0 * basal[0] + speed1 * basal[1])
    hess[my_rows, :] = action
    vbs[0, my_rows, :] = action
    for o in range(1, ngz):
        send_back(2, o, vbs.at[0, my_rows, :])
    for copy in finals:
        copy.wait()
    for copy in rest:
        copy.wait()
    for group in incoming:
        for copy in group:
            copy.wait_send()
    for copy in halo0 + halo1 + halo2 + halo3 + reductions:
        copy.wait_send()


def deliver(inc_in, adj_in, hess_in, inc, adj, hess, first, second, third, sem):
    held = ((inc_in, first, inc), (adj_in, second, adj), (hess_in, third, hess))
    reads = [pltpu.make_async_copy(src, mid, sem.at[n]) for n, (src, mid, _) in enumerate(held)]
    writes = [pltpu.make_async_copy(mid, dst, sem.at[n + 3]) for n, (_, mid, dst) in enumerate(held)]
    for copy in reads:
        copy.start()
    for read, write in zip(reads, writes):
        read.wait()
        write.start()
    for copy in writes:
        copy.wait()


def local(sizes, *args):
    ngx, ngy, ngz = sizes
    field = pltpu.VMEM((NZ, ROWS, LANES), F32)
    state = pltpu.VMEM((2, NZ + 2, ROWS, LANES), F32)
    depth, rows, lanes = args[1].shape
    dma = pltpu.SemaphoreType.DMA

    def halo(length, packs):
        return [pltpu.VMEM((2, length, LANES), F32)] * 2 + [pltpu.VMEM((2, packs * ROWS, LANES), F32)] * 2

    na, nb = ngx * 2, (ngy // 2) * ngz
    scratch = (
        [pltpu.VMEM((2, depth, rows, lanes), F32), pltpu.VMEM((rows, lanes), jnp.int32)]
        + [pltpu.VMEM((ROWS, LANES), F32)] * 3
        + [pltpu.VMEM((NZ + 1, ROWS, LANES), F32), pltpu.VMEM((3, NZ, ROWS, LANES), F32), field]
        + [pltpu.VMEM((2, rows, lanes), F32), pltpu.VMEM((ngz, 2, ROWS, LANES), F32)]
        + [pltpu.VMEM((NZ + 1, ROWS, LANES), F32)]
        + [field] * 6
        + [state] * 6
        + halo(NZ + 8, 1) + halo(4 * NZ, 1) + halo(6 * NZ, 2) + halo(2 * NZ, 1)
        + [pltpu.VMEM((2, ROWS, LANES), F32), pltpu.VMEM((2, 2, 1, LANES), F32)]
        + [pltpu.VMEM((2, na, 1, LANES), F32), pltpu.VMEM((2, nb, 1, LANES), F32)]
        + [dma((5,)), dma((4,)), dma((4, ngz)), dma((4, ngz)), dma((4, 4)), dma((4, 4))]
        + [dma((2, 2, max(na, nb))), dma((2, na)), dma((2, nb)), dma((3, ngz)), dma((3, ngz))]
    )
    vmem = pl.BlockSpec(memory_space=pltpu.VMEM)
    hbm = pl.BlockSpec(memory_space=pl.ANY)
    smem = pl.BlockSpec(memory_space=pltpu.SMEM)
    shapes = (
        jax.ShapeDtypeStruct((2, depth, rows, lanes), F32),
        jax.ShapeDtypeStruct((2, depth, rows, lanes), F32),
        jax.ShapeDtypeStruct((rows, lanes), F32),
    )
    results = pl.pallas_call(
        functools.partial(kernel, sizes),
        out_shape=shapes,
        in_specs=[hbm] * 7 + [smem, hbm],
        out_specs=(hbm, hbm, vmem),
        scratch_shapes=scratch,
        compiler_params=pltpu.CompilerParams(
            collective_id=0, has_side_effects=True, vmem_limit_bytes=62 * 1024 * 1024
        ),
    )(*args)
    return pl.pallas_call(
        deliver,
        out_shape=shapes,
        in_specs=[hbm] * 3,
        out_specs=(hbm, hbm, hbm),
        scratch_shapes=[pltpu.VMEM(shape.shape, F32) for shape in shapes] + [dma((6,))],
        compiler_params=pltpu.CompilerParams(vmem_limit_bytes=62 * 1024 * 1024),
    )(*results)


def solution(mesh):
    sizes = (mesh.shape["gx"], mesh.shape["gy"], mesh.shape["gz"])
    wide, cell, flat = P(None, "gz", "gx", "gy"), P("gz", "gx", "gy"), P("gx", "gy")
    return jax.shard_map(
        functools.partial(local, sizes),
        mesh=mesh,
        in_specs=(wide, cell, wide, cell, flat, flat, flat, flat, flat),
        out_specs=(wide, wide, flat),
        check_vma=False,
    )
```

```python
import functools

import jax
import jax.numpy as jnp
from jax import lax
from jax.experimental import pallas as pl
from jax.experimental.pallas import tpu as pltpu
from jax.sharding import PartitionSpec as P

TILE = 16
VERTICAL = 8.0
STRETCH = 4.0
NONE = 1000.0
MESH = pl.DeviceIdType.MESH
F32 = jnp.float32
NZ = 32
ROWS = 16
LANES = 128
UNROLL = 32


def blocked_loop(steps, body, carry):
    def chunk(index, state):
        for inner in range(UNROLL):
            state = body(index * UNROLL + inner, state)
        return state

    return lax.fori_loop(0, steps // UNROLL, chunk, carry)


def kernel(
    sizes,
    vel_in, visc, binv, coup, fric_in, fstep_in, misfit_in, ice, bed_in,
    inc, adj, hess,
    vel, bed, fric, fstep, misfit,
    FX, V, B, L, vbs, vbp, WU, WE, WW, WN, WS, D0, D1,
    Z0, ZA, S0, SA, ZB, SB,
    xs0, xr0, ps0, pr0, xs1, xr1, ps1, pr1, xs2, xr2, ps2, pr2, xs3, xr3, ps3, pr3,
    stack, rt, ra, rb,
    gathered, load_sem, loc_sem, in_send, in_recv, halo_send, halo_recv, red_send, red_recv_a, red_recv_b,
    out_send, out_recv,
):
    ngx, ngy, ngz = sizes
    gx, gy, gz = lax.axis_index("gx"), lax.axis_index("gy"), lax.axis_index("gz")
    depth = NZ // ngz
    odd = lax.rem(gx, 2)

    def around(index, count):
        return [index] + [lax.rem(index + o, count) for o in range(1, count)]

    def piece_of(q):
        return q + odd * (ngz - 1 - 2 * q)

    gxs, gzs = around(gx, ngx), around(gz, ngz)
    pieces = [piece_of(q) for q in gzs]
    piece = pieces[0]
    total_pieces = ngx * ngz
    spot = gx * ngz + piece

    def holder(index):
        block = lax.div(index, ngz)
        part = index - block * ngz
        return (block, gy, part + lax.rem(block, 2) * (ngz - 1 - 2 * part))

    x_low = holder(lax.rem(spot + (total_pieces - 1), total_pieces))
    x_high = holder(lax.rem(spot + 1, total_pieces))
    y_low = (gx, lax.rem(gy + (ngy - 1), ngy), gz)
    y_high = (gx, lax.rem(gy + 1, ngy), gz)
    peers = [(gx, gy, q) for q in gzs[1:]]
    chips = ngy // 2
    na, nb = ngx * 2, chips * ngz
    chip = lax.div(gy, 2)
    core = gy - 2 * chip
    same_core = [2 * c + core for c in around(chip, chips)]
    other_core = 2 * chip + 1 - core
    ma, mb = gx * 2 + core, chip * ngz + gz
    y_other = (gx, lax.rem(gy + ngy + 2 * core - 1, ngy), gz)

    def ring(offset, count):
        return min(offset, count - offset)

    steps_a = sorted(
        ((i, j) for i in range(ngx) for j in range(2) if i or j), key=lambda step: -ring(step[0], ngx)
    )
    steps_b = sorted(
        ((i, j) for i in range(chips) for j in range(ngz) if i or j),
        key=lambda step: -ring(step[0], chips) - ring(step[1], ngz),
    )
    group_a = [(gxs[i], other_core if j else gy, gz) for i, j in steps_a]
    group_b = [(gx, same_core[i], gzs[j]) for i, j in steps_b]

    here = pl.multiple_of(piece * ROWS, ROWS)
    my_rows = pl.ds(here, ROWS)
    loads = []
    for n, (src, dst) in enumerate(
        [
            (bed_in, bed),
            (vel_in, vel),
            (fric_in.at[my_rows, :], fric),
            (fstep_in.at[my_rows, :], fstep),
            (misfit_in.at[my_rows, :], misfit),
        ]
    ):
        copy = pltpu.make_async_copy(src, dst, load_sem.at[n])
        copy.start()
        loads.append(copy)

    barrier = pltpu.get_barrier_semaphore()
    far = [(-ring(i, ngx), device) for (i, _), device in zip(steps_a, group_a)]
    far += [(-ring(i, chips) - ring(j, ngz), device) for (i, j), device in zip(steps_b, group_b)]
    partners = [device for _, device in sorted(far, key=lambda item: item[0])] + [y_other]
    for partner in partners:
        pl.semaphore_signal(barrier, inc=1, device_id=partner, device_id_type=MESH)

    base = gz * depth
    for copy in loads:
        copy.wait()
    bedf = bed[...]
    vb0 = jnp.zeros(bedf.shape, F32)
    vb1 = jnp.zeros(bedf.shape, F32)
    for k in range(depth):
        at = bedf == base + k
        vb0 = jnp.where(at, vel[0, k], vb0)
        vb1 = jnp.where(at, vel[1, k], vb1)
    vbs[0] = vb0
    vbs[1] = vb1

    pl.semaphore_wait(barrier, len(partners))

    layers = pl.ds(base, depth)

    def moves(part, o):
        rows = pl.ds(pl.multiple_of(part * ROWS, ROWS), ROWS)
        return [
            (visc.at[:, rows, :], V.at[layers]),
            (binv.at[:, :, rows, :], B.at[:, layers]),
            (coup.at[:, rows, :], L.at[layers]),
            (vbs.at[:, rows, :], vbp.at[o]),
        ]

    locals_in = []
    for a, (src, dst) in enumerate(moves(piece, 0)):
        copy = pltpu.make_async_copy(src, dst, loc_sem.at[a])
        copy.start()
        locals_in.append(copy)
    incoming = [[], [], [], []]
    per_peer = [moves(pieces[o], o) for o in range(1, ngz)]
    for a in (3, 1, 2, 0):
        for o in range(1, ngz):
            src, dst = per_peer[o - 1][a]
            copy = pltpu.make_async_remote_copy(
                src_ref=src, dst_ref=dst,
                send_sem=in_send.at[a, o], recv_sem=in_recv.at[a, o],
                device_id=peers[o - 1], device_id_type=MESH,
            )
            copy.start()
            incoming[a].append(copy)

    row = lax.broadcasted_iota(jnp.int32, (ROWS, LANES), 0)
    lane = lax.broadcasted_iota(jnp.int32, (ROWS, LANES), 1)
    column = jnp.zeros((ROWS, LANES), F32)
    for j in range(LANES // TILE):
        flag = ice[piece, j].astype(F32)
        column = jnp.where(lane // TILE == j, flag, column)
    has_ice = column > 0.5
    kbed = jnp.where(has_ice, bed[my_rows, :].astype(F32), NONE)
    friction = fric[...]
    load = misfit[...] * column

    for field in (Z0, ZA, S0, SA, ZB, SB):
        for c in range(2):
            field[c, 0] = jnp.zeros((ROWS, LANES), F32)
            field[c, NZ + 1] = jnp.zeros((ROWS, LANES), F32)
    V[NZ] = jnp.zeros((ROWS, LANES), F32)
    for ps in (ps0, ps3):
        ps[...] = jnp.zeros(ps.shape, F32)

    def pack_lane(packed, value, j):
        low, high = packed
        low = jnp.where(lane == j, pltpu.roll(value, j, 1), low)
        high = jnp.where(lane == j, pltpu.roll(value, (j + 1) % LANES, 1), high)
        return low, high

    def pack_rows(xs, value, j):
        xs[0, pl.ds(j, 1), :] = value[0:1, :]
        xs[1, pl.ds(j, 1), :] = value[ROWS - 1 : ROWS, :]

    def send_halo(index, xs, xr, ps, pr):
        copies = []
        for side, (src, dst, device) in enumerate(
            [
                (ps.at[0], pr.at[1], y_low),
                (ps.at[1], pr.at[0], y_high),
                (xs.at[0], xr.at[1], x_low),
                (xs.at[1], xr.at[0], x_high),
            ]
        ):
            copy = pltpu.make_async_remote_copy(
                src_ref=src, dst_ref=dst,
                send_sem=halo_send.at[index, side], recv_sem=halo_recv.at[index, side],
                device_id=device, device_id_type=MESH,
            )
            copy.start()
            copies.append(copy)
        return copies

    blank = jnp.zeros((ROWS, LANES), F32)
    for group, copy in zip(incoming[1:], locals_in[1:]):
        copy.wait()
        for remote in group:
            remote.wait_recv()
    speed0 = vbp[0, 0]
    speed1 = vbp[0, 1]
    for o in range(1, ngz):
        speed0 = speed0 + vbp[o, 0]
        speed1 = speed1 + vbp[o, 1]
    speed0 = jnp.where(has_ice, speed0, 0.0)
    speed1 = jnp.where(has_ice, speed1, 0.0)
    drive = friction * fstep[...]
    push0, push1 = drive * speed0, drive * speed1

    def apply_inverse(k, first, second):
        b0, b1, b2 = B[0, k], B[1, k], B[2, k]
        return b0 * first + b1 * second, b1 * first + b2 * second

    def rise(k, first, second, state, out):
        y0, y1, total = state
        link = L[k]
        t0 = first + link * y0
        t1 = second + link * y1
        y0, y1 = apply_inverse(k, t0, t1)
        out[0, k + 1] = y0
        out[1, k + 1] = y1
        return y0, y1, total + (t0 * y0 + t1 * y1)

    def first_rise(k, state):
        level = jnp.full((ROWS, LANES), k, jnp.int32).astype(F32)
        act = jnp.where(level >= kbed, 1.0, 0.0)
        beneath = jnp.where(level - 1.0 >= kbed, 1.0, 0.0)
        rest = 1.0 - act
        B[0, k] = act * B[0, k] + rest
        B[1, k] = act * B[1, k]
        B[2, k] = act * B[2, k] + rest
        L[k] = L[k] * act * beneath
        at = level == kbed
        first = jnp.where(at, push0, 0.0)
        second = jnp.where(at, push1, 0.0)
        return rise(k, first, second, state, Z0)

    state = blocked_loop(NZ, first_rise, (blank, blank, blank))
    rz0 = state[2]

    def fall(k, g0, g1, field):
        add0, add1 = apply_inverse(k, g0, g1)
        z0 = field[0, k + 1] + add0
        z1 = field[1, k + 1] + add1
        field[0, k + 1] = z0
        field[1, k + 1] = z1
        link = L[k]
        return z0, z1, link * z0, link * z1

    def fall_bare(k, g0, g1, field):
        z0, z1 = apply_inverse(k, g0, g1)
        field[0, k + 1] = z0
        field[1, k + 1] = z1
        link = L[k]
        return z0, z1, link * z0, link * z1

    seed_a0, seed_a1 = load * Z0[0, NZ], load * Z0[1, NZ]

    def fall_first(i, carry):
        k = NZ - 1 - i
        g0, g1, a0, a1, low, high = carry
        z0, z1, g0, g1 = fall(k, g0, g1, Z0)
        y0, y1, a0, a1 = fall_bare(k, a0, a1, ZA)
        packed = (low, high)
        for n, value in enumerate((z0, z1, y0, y1)):
            pack_rows(xs1, value, k + NZ * n)
            packed = pack_lane(packed, value, k + NZ * n)
        return (g0, g1, a0, a1) + packed

    carry = blocked_loop(NZ, fall_first, (blank, blank, seed_a0, seed_a1, blank, blank))
    ps1[0] = carry[4]
    ps1[1] = carry[5]
    halo1 = send_halo(1, xs1, xr1, ps1, pr1)
    raa = seed_a0 * ZA[0, NZ] + seed_a1 * ZA[1, NZ]

    locals_in[0].wait()
    for copy in incoming[0]:
        copy.wait_recv()

    def pack_viscosity(k, packed):
        value = V[k]
        pack_rows(xs0, value, k)
        return pack_lane(packed, value, k)

    packed = blocked_loop(NZ, pack_viscosity, (blank, blank))
    pack_rows(xs0, kbed, NZ)
    low, high = pack_lane(packed, kbed, NZ)
    ps0[0] = low
    ps0[1] = high
    halo0 = send_halo(0, xs0, xr0, ps0, pr0)

    def beside(value):
        east = pltpu.roll(value, ROWS - 1, 0)
        west = pltpu.roll(value, 1, 0)
        north = pltpu.roll(value, LANES - 1, 1)
        south = pltpu.roll(value, 1, 1)
        return east, west, north, south

    bed_e, bed_w, bed_n, bed_s = beside(kbed)
    bed_e = jnp.where(row == ROWS - 1, NONE, bed_e)
    bed_w = jnp.where(row == 0, NONE, bed_w)
    bed_n = jnp.where(lane == LANES - 1, NONE, bed_n)
    bed_s = jnp.where(lane == 0, NONE, bed_s)

    def layer_weights(k, down):
        level = jnp.full((ROWS, LANES), k, jnp.int32).astype(F32)
        value = V[k]
        act = jnp.where(level >= kbed, 1.0, 0.0)
        above = jnp.where((level + 1.0 >= kbed) & (level + 1.0 < NZ), 1.0, 0.0)
        bedflag = jnp.where(level == kbed, 1.0, 0.0)
        east, west, north, south = beside(value)
        half_act = 0.5 * act
        up = (VERTICAL * (value + V[k + 1])) * (half_act * above)
        we = (value + east) * jnp.where(level >= bed_e, half_act, 0.0)
        ww = (value + west) * jnp.where(level >= bed_w, half_act, 0.0)
        wn = (value + north) * jnp.where(level >= bed_n, half_act, 0.0)
        ws = (value + south) * jnp.where(level >= bed_s, half_act, 0.0)
        WU[k + 1] = up
        WE[k] = we
        WW[k] = ww
        WN[k] = wn
        WS[k] = ws
        ew, ns = we + ww, wn + ws
        rest = (up + down) + friction * bedflag + (1.0 - act)
        D0[k] = STRETCH * ew + ns + rest
        D1[k] = ew + STRETCH * ns + rest
        return up

    WU[0] = blank
    blocked_loop(NZ, layer_weights, blank)

    def operate(k, weights, field):
        up, down, we, ww, wn, ws, d0, d1 = weights
        result = []
        for c in range(2):
            value = field[c, k + 1]
            east, west, north, south = beside(value)
            vertical = up * field[c, k + 2] + down * field[c, k]
            ew = we * east + ww * west
            ns = wn * north + ws * south
            if c == 0:
                result.append(d0 * value - vertical - STRETCH * ew - ns)
            else:
                result.append(d1 * value - vertical - ew - STRETCH * ns)
        return result

    def keep(k, weights, field, out):
        image = operate(k, weights, field)
        out[0, k + 1] = image[0]
        out[1, k + 1] = image[1]

    def complete(k, inner, xr, low, high, n, lanes_from):
        return [
            inner[c, k + 1] + shared(xr, NZ * (n + c) + k, low, high, lanes_from + NZ * c + k)
            for c in range(2)
        ]

    def weights_of(k):
        return WU[k + 1], WU[k], WE[k], WW[k], WN[k], WS[k], D0[k], D1[k]

    def against(field, k, image, total):
        return total + (field[0, k + 1] * image[0] + field[1, k + 1] * image[1])

    def inner_first(k, carry):
        weights = weights_of(k)
        keep(k, weights, Z0, S0)
        keep(k, weights, ZA, SA)
        return carry

    blocked_loop(NZ, inner_first, 0)
    for copy in halo0:
        copy.wait_recv()
    rows_level = lax.broadcasted_iota(jnp.int32, (NZ, LANES), 0).astype(F32)
    lanes_level = lane.astype(F32)
    x_edges = (spot == 0, spot == total_pieces - 1)
    y_edges = (gy == 0, gy == ngy - 1)
    FY = []
    for side in range(2):
        own_bed = xs0[side, NZ : NZ + 1, :]
        their_bed = jnp.where(x_edges[side], NONE, xr0[side, NZ : NZ + 1, :])
        both = (rows_level >= own_bed) & (rows_level >= their_bed)
        face = jnp.where(both, 0.5 * (xs0[side, :NZ, :] + xr0[side, :NZ, :]), 0.0)
        FX[side, :NZ, :] = STRETCH * face
        FX[side, NZ:, :] = face
        own, theirs = ps0[side], pr0[side]
        own_bed = jnp.sum(jnp.where(lane == NZ, own, 0.0), axis=1, keepdims=True)
        their_bed = jnp.sum(jnp.where(lane == NZ, theirs, 0.0), axis=1, keepdims=True)
        their_bed = jnp.where(y_edges[side], NONE, their_bed)
        both = (lanes_level >= own_bed) & (lanes_level >= their_bed) & (lane < NZ)
        face = jnp.where(both, 0.5 * (own + theirs), 0.0)
        face = face + STRETCH * pltpu.roll(face, NZ, 1)
        FY.append(face + pltpu.roll(face, 2 * NZ, 1))

    def exchange(xs, xr, ps, pr, fields, packs):
        for side in range(2):
            for n in range(fields):
                part = pl.ds(2 * NZ * n, 2 * NZ)
                xr[side, part, :] = FX[side] * (xs[side, part, :] - xr[side, part, :])
            for n in range(packs):
                part = pl.ds(ROWS * n, ROWS)
                pr[side, part, :] = FY[side] * (ps[side, part, :] - pr[side, part, :])

    def shared(xr, xj, low, high, lj):
        result = jnp.where(row == 0, xr[0, pl.ds(xj, 1), :], 0.0)
        result = jnp.where(row == ROWS - 1, xr[1, pl.ds(xj, 1), :], result)
        result = result + jnp.where(lane == 0, pltpu.roll(low, lax.rem(LANES - lj, LANES), 1), 0.0)
        return result + jnp.where(lane == LANES - 1, pltpu.roll(high, LANES - 1 - lj, 1), 0.0)

    def shared_energy(xs, ps, first, pack, start, xr, pr, xr_first, pr_pack, pr_start):
        total = blank
        for side in range(2):
            for n in range(2 * NZ // ROWS):
                mine = xs[side, pl.ds(2 * NZ * first + ROWS * n, ROWS), :]
                total = total + mine * xr[side, pl.ds(2 * NZ * xr_first + ROWS * n, ROWS), :]
            mine = ps[side, pl.ds(ROWS * pack, ROWS), :]
            theirs = pr[side, pl.ds(ROWS * pr_pack, ROWS), :]
            if start != pr_start:
                mine = pltpu.roll(mine, (pr_start - start) % LANES, 1)
            inside = (lane >= pr_start) & (lane < pr_start + 2 * NZ)
            total = total + jnp.where(inside, mine * theirs, 0.0)
        return total

    for copy in halo1:
        copy.wait_recv()
    exchange(xs1, xr1, ps1, pr1, 2, 1)
    low1, high1 = pr1[0], pr1[1]

    def middle_rise(k, carry):
        pq0, paa, main, extra = carry
        w = complete(k, S0, xr1, low1, high1, 0, 0)
        wa = complete(k, SA, xr1, low1, high1, 2, 2 * NZ)
        pq0 = against(Z0, k, w, pq0)
        paa = against(ZA, k, wa, paa)
        main = rise(k, w[0], w[1], main, S0)
        extra = rise(k, wa[0], wa[1], extra, SA)
        return pq0, paa, main, extra

    triple = (blank, blank, blank)
    pq0, paa, main, extra = blocked_loop(NZ, middle_rise, (blank, blank, triple, triple))
    g0, gaa = main[2], extra[2]
    seed_b0, seed_b1 = load * S0[0, NZ], load * S0[1, NZ]

    def fall_second(i, carry):
        k = NZ - 1 - i
        g0, g1, h0, h1, b0, b1, low1, high1, low2, high2 = carry
        z0, z1, g0, g1 = fall(k, g0, g1, S0)
        a0, a1, h0, h1 = fall(k, h0, h1, SA)
        y0, y1, b0, b1 = fall_bare(k, b0, b1, ZB)
        packed = (low1, high1)
        for n, value in enumerate((y0, y1, z0, z1)):
            pack_rows(xs2, value, k + NZ * n)
            packed = pack_lane(packed, value, k + NZ * n)
        other = (low2, high2)
        for n, value in enumerate((a0, a1)):
            pack_rows(xs2, value, k + NZ * (n + 4))
            other = pack_lane(other, value, k + NZ * n)
        return (g0, g1, h0, h1, b0, b1) + packed + other

    carry = blocked_loop(
        NZ, fall_second, (blank, blank, blank, blank, seed_b0, seed_b1, blank, blank, blank, blank)
    )
    for n in range(2):
        ps2[0, ROWS * n : ROWS * (n + 1), :] = carry[6 + 2 * n]
        ps2[1, ROWS * n : ROWS * (n + 1), :] = carry[7 + 2 * n]
    halo2 = send_halo(2, xs2, xr2, ps2, pr2)
    rab = seed_a0 * ZB[0, NZ] + seed_a1 * ZB[1, NZ]
    rbb = seed_b0 * ZB[0, NZ] + seed_b1 * ZB[1, NZ]

    def inner_second(k, carry):
        d0, daa = carry
        weights = weights_of(k)
        keep(k, weights, ZB, SB)
        d0 = against(S0, k, operate(k, weights, S0), d0)
        daa = against(SA, k, operate(k, weights, SA), daa)
        return d0, daa

    d0, daa = blocked_loop(NZ, inner_second, (blank, blank))
    for copy in halo2:
        copy.wait_recv()
    exchange(xs2, xr2, ps2, pr2, 3, 2)
    low2, high2 = pr2[0, :ROWS, :], pr2[1, :ROWS, :]

    def last_rise(k, carry):
        pab, pbb, gab, main = carry
        w = complete(k, SB, xr2, low2, high2, 0, 0)
        pab = against(ZA, k, w, pab)
        pbb = against(ZB, k, w, pbb)
        gab = against(SA, k, w, gab)
        main = rise(k, w[0], w[1], main, SB)
        return pab, pbb, gab, main

    pab, pbb, gab, main = blocked_loop(NZ, last_rise, (blank, blank, blank, triple))
    gbb = main[2]

    def fall_third(i, carry):
        k = NZ - 1 - i
        g0, g1, low, high = carry
        z0, z1, g0, g1 = fall(k, g0, g1, SB)
        packed = (low, high)
        for n, value in enumerate((z0, z1)):
            pack_rows(xs3, value, k + NZ * n)
            packed = pack_lane(packed, value, k + NZ * n)
        return (g0, g1) + packed

    carry = blocked_loop(NZ, fall_third, (blank, blank, blank, blank))
    ps3[0] = carry[2]
    ps3[1] = carry[3]
    halo3 = send_halo(3, xs3, xr3, ps3, pr3)

    finals = []
    rest = []
    places = [
        gathered.at[0, :, :, my_rows, :],
        gathered.at[1, :, :, my_rows, :],
        adj.at[:, :, my_rows, :],
        hess.at[my_rows, :],
    ]

    def give_back(n, field):
        for o in range(1, ngz):
            send_back(n, o, field.at[:, pl.ds(1 + gzs[o] * depth, depth)])
        copy = pltpu.make_async_copy(field.at[:, pl.ds(1 + base, depth)], places[n], loc_sem.at[n])
        copy.start()
        finals.append(copy)

    def send_back(n, o, src):
        copy = pltpu.make_async_remote_copy(
            src_ref=src, dst_ref=places[n],
            send_sem=out_send.at[n, o], recv_sem=out_recv.at[n, o],
            device_id=peers[o - 1], device_id_type=MESH,
        )
        copy.start()
        rest.append(copy)

    give_back(0, Z0)
    give_back(1, S0)
    d0 = d0 + shared_energy(xs2, ps2, 1, 0, 2 * NZ, xr2, pr2, 1, 0, 2 * NZ)
    daa = daa + shared_energy(xs2, ps2, 2, 1, 0, xr2, pr2, 2, 1, 0)

    stages = ((group_a, ra, red_recv_a, ma), (group_b, rb, red_recv_b, mb))

    def gather_sums(values, turn):
        for n, value in enumerate(values):
            stack[turn, n : n + 1, :] = jnp.sum(value, axis=0, keepdims=True)
        each = jnp.sum(stack[turn], axis=1, keepdims=True)
        return jnp.sum(jnp.where(lane == row, each, 0.0), axis=0, keepdims=True)

    def send_sum(turn, stage, value):
        rt[turn, stage] = value
        group, received, sem, place = stages[stage]
        received[turn, place] = value
        copies = []
        for o, device in enumerate(group):
            copy = pltpu.make_async_remote_copy(
                src_ref=rt.at[turn, stage], dst_ref=received.at[turn, place],
                send_sem=red_send.at[turn, stage, o], recv_sem=sem.at[turn, o],
                device_id=device, device_id_type=MESH,
            )
            copy.start()
            copies.append(copy)
        return copies

    def finish_sum(turn, stage, copies):
        for copy in copies:
            copy.wait_recv()
        received = stages[stage][1]
        return jnp.sum(received[turn], axis=0)

    def spread(total, count):
        each = jnp.sum(jnp.where(lane == row, total, 0.0), axis=1, keepdims=True)
        each = jnp.broadcast_to(each, (ROWS, LANES))
        return [each[n : n + 1, :] for n in range(count)]

    stack[...] = jnp.zeros(stack.shape, F32)
    first_a = send_sum(0, 0, gather_sums([rz0, pq0, g0, d0], 0))

    def inner_third(k, carry):
        dab, dbb = carry
        image = operate(k, weights_of(k), SB)
        return against(SA, k, image, dab), against(SB, k, image, dbb)

    dab, dbb = blocked_loop(NZ, inner_third, (blank, blank))
    for copy in halo3:
        copy.wait_recv()
    exchange(xs3, xr3, ps3, pr3, 1, 1)
    dab = dab + shared_energy(xs2, ps2, 2, 1, 0, xr3, pr3, 0, 0, 0)
    dbb = dbb + shared_energy(xs3, ps3, 0, 0, 0, xr3, pr3, 0, 0, 0)
    second_a = send_sum(
        1, 0, gather_sums([raa, rab, rbb, paa, pab, pbb, gaa, gab, gbb, daa, dab, dbb], 1)
    )
    first_b = send_sum(0, 1, finish_sum(0, 0, first_a))
    second_b = send_sum(1, 1, finish_sum(1, 0, second_a))
    reductions = first_a + second_a + first_b + second_b
    rz0, pq0, g0, d0 = spread(finish_sum(0, 1, first_b), 4)

    def combination(rz, pq, g, d):
        step = rz / pq
        renewed = step * step * g - rz
        grow = 1.0 + renewed / rz
        energy = grow * grow * pq - 2.0 * grow * step * g + step * step * d
        second = renewed / energy
        return step + second * grow, -(second * step)

    c0, c1 = combination(rz0, pq0, g0, d0)

    for copy in finals:
        copy.wait()
    for copy in rest:
        copy.wait_recv()

    def increments(k, carry):
        for c in range(2):
            gathered[0, c, k] = c0 * gathered[0, c, k] + c1 * gathered[1, c, k]
        return carry

    lax.fori_loop(0, depth, increments, 0)
    landed = len(rest)
    finals = [pltpu.make_async_copy(gathered.at[0], inc, loc_sem.at[3])]
    finals[0].start()

    raa, rab, rbb, paa, pab, pbb, gaa, gab, gbb, daa, dab, dbb = spread(finish_sum(1, 1, second_b), 12)

    def form(aa, ab, bb):
        return c0 * c0 * aa + 2.0 * (c0 * c1) * ab + c1 * c1 * bb

    e0, e1 = combination(form(raa, rab, rbb), form(paa, pab, pbb), form(gaa, gab, gbb), form(daa, dab, dbb))
    f_za, f_zb, f_sa, f_sb = e0 * c0, e0 * c1, e1 * c0, e1 * c1

    def adjoints(k, carry):
        level = jnp.full((ROWS, LANES), k, jnp.int32).astype(F32)
        at = level == kbed
        out = []
        for c in range(2):
            value = (f_za * ZA[c, k + 1] + f_zb * ZB[c, k + 1]) + (f_sa * SA[c, k + 1] + f_sb * SB[c, k + 1])
            ZA[c, k + 1] = value
            out.append(jnp.where(at, value, carry[c]))
        return tuple(out)

    basal = blocked_loop(NZ, adjoints, (blank, blank))
    give_back(2, ZA)
    action = friction * (speed0 * basal[0] + speed1 * basal[1])
    hess[my_rows, :] = action
    vbs[0, my_rows, :] = action
    for o in range(1, ngz):
        send_back(3, o, vbs.at[0, my_rows, :])
    for copy in finals:
        copy.wait()
    for copy in rest[landed:]:
        copy.wait_recv()
    for copy in rest:
        copy.wait_send()
    for group in incoming:
        for copy in group:
            copy.wait_send()
    for copy in halo0 + halo1 + halo2 + halo3 + reductions:
        copy.wait_send()


def deliver(inc_in, adj_in, hess_in, inc, adj, hess, first, second, third, sem):
    held = ((inc_in, first, inc), (adj_in, second, adj), (hess_in, third, hess))
    reads = [pltpu.make_async_copy(src, mid, sem.at[n]) for n, (src, mid, _) in enumerate(held)]
    writes = [pltpu.make_async_copy(mid, dst, sem.at[n + 3]) for n, (_, mid, dst) in enumerate(held)]
    for copy in reads:
        copy.start()
    for read, write in zip(reads, writes):
        read.wait()
        write.start()
    for copy in writes:
        copy.wait()


def local(sizes, *args):
    ngx, ngy, ngz = sizes
    field = pltpu.VMEM((NZ, ROWS, LANES), F32)
    state = pltpu.VMEM((2, NZ + 2, ROWS, LANES), F32)
    depth, rows, lanes = args[1].shape
    dma = pltpu.SemaphoreType.DMA

    def halo(length, packs):
        return [pltpu.VMEM((2, length, LANES), F32)] * 2 + [pltpu.VMEM((2, packs * ROWS, LANES), F32)] * 2

    na, nb = ngx * 2, (ngy // 2) * ngz
    scratch = (
        [pltpu.VMEM((2, depth, rows, lanes), F32), pltpu.VMEM((rows, lanes), jnp.int32)]
        + [pltpu.VMEM((ROWS, LANES), F32)] * 3
        + [pltpu.VMEM((2, 2 * NZ, LANES), F32)]
        + [pltpu.VMEM((NZ + 1, ROWS, LANES), F32), pltpu.VMEM((3, NZ, ROWS, LANES), F32), field]
        + [pltpu.VMEM((2, rows, lanes), F32), pltpu.VMEM((ngz, 2, ROWS, LANES), F32)]
        + [pltpu.VMEM((NZ + 1, ROWS, LANES), F32)]
        + [field] * 6
        + [state] * 6
        + halo(NZ + 8, 1) + halo(4 * NZ, 1) + halo(6 * NZ, 2) + halo(2 * NZ, 1)
        + [pltpu.VMEM((2, ROWS, LANES), F32), pltpu.VMEM((2, 2, 1, LANES), F32)]
        + [pltpu.VMEM((2, na, 1, LANES), F32), pltpu.VMEM((2, nb, 1, LANES), F32)]
        + [pltpu.VMEM((2, 2, depth, rows, lanes), F32)]
        + [dma((5,)), dma((4,)), dma((4, ngz)), dma((4, ngz)), dma((4, 4)), dma((4, 4))]
        + [dma((2, 2, max(na, nb))), dma((2, na)), dma((2, nb)), dma((4, ngz)), dma((4, ngz))]
    )
    vmem = pl.BlockSpec(memory_space=pltpu.VMEM)
    hbm = pl.BlockSpec(memory_space=pl.ANY)
    smem = pl.BlockSpec(memory_space=pltpu.SMEM)
    shapes = (
        jax.ShapeDtypeStruct((2, depth, rows, lanes), F32),
        jax.ShapeDtypeStruct((2, depth, rows, lanes), F32),
        jax.ShapeDtypeStruct((rows, lanes), F32),
    )
    results = pl.pallas_call(
        functools.partial(kernel, sizes),
        out_shape=shapes,
        in_specs=[hbm] * 7 + [smem, hbm],
        out_specs=(hbm, hbm, vmem),
        scratch_shapes=scratch,
        compiler_params=pltpu.CompilerParams(
            collective_id=0, has_side_effects=True, vmem_limit_bytes=62 * 1024 * 1024
        ),
    )(*args)
    return pl.pallas_call(
        deliver,
        out_shape=shapes,
        in_specs=[hbm] * 3,
        out_specs=(hbm, hbm, hbm),
        scratch_shapes=[pltpu.VMEM(shape.shape, F32) for shape in shapes] + [dma((6,))],
        compiler_params=pltpu.CompilerParams(vmem_limit_bytes=62 * 1024 * 1024),
    )(*results)


def solution(mesh):
    sizes = (mesh.shape["gx"], mesh.shape["gy"], mesh.shape["gz"])
    wide, cell, flat = P(None, "gz", "gx", "gy"), P("gz", "gx", "gy"), P("gx", "gy")
    return jax.shard_map(
        functools.partial(local, sizes),
        mesh=mesh,
        in_specs=(wide, cell, wide, cell, flat, flat, flat, flat, flat),
        out_specs=(wide, wide, flat),
        check_vma=False,
    )
```

```python
import functools

import jax
import jax.numpy as jnp
from jax import lax
from jax.experimental import pallas as pl
from jax.experimental.pallas import tpu as pltpu
from jax.sharding import PartitionSpec as P

TILE = 16
VERTICAL = 8.0
STRETCH = 4.0
NONE = 1000.0
MESH = pl.DeviceIdType.MESH
F32 = jnp.float32
NZ = 32
ROWS = 16
LANES = 128
UNROLL = 32


def blocked_loop(steps, body, carry):
    def chunk(index, state):
        for inner in range(UNROLL):
            state = body(index * UNROLL + inner, state)
        return state

    return lax.fori_loop(0, steps // UNROLL, chunk, carry)


def kernel(
    sizes,
    vel_in, visc, binv, coup, fric_in, fstep_in, misfit_in, ice, bed_in,
    inc, adj, hess,
    vel, bed, fric, fstep, misfit,
    FX, V, B, L, vbs, vbp, WU, WE, WW, WN, WS, D0, D1,
    Z0, ZA, S0, SA, ZB, SB,
    xs0, xr0, ps0, pr0, xs1, xr1, ps1, pr1, xs2, xr2, ps2, pr2, xs3, xr3, ps3, pr3,
    stack, rt, ra, rb,
    gathered, load_sem, loc_sem, in_send, in_recv, halo_send, halo_recv, red_send, red_recv_a, red_recv_b,
    out_send, out_recv,
):
    ngx, ngy, ngz = sizes
    gx, gy, gz = lax.axis_index("gx"), lax.axis_index("gy"), lax.axis_index("gz")
    depth = NZ // ngz
    odd = lax.rem(gx, 2)

    def around(index, count):
        return [index] + [lax.rem(index + o, count) for o in range(1, count)]

    def piece_of(q):
        return q + odd * (ngz - 1 - 2 * q)

    gxs, gzs = around(gx, ngx), around(gz, ngz)
    pieces = [piece_of(q) for q in gzs]
    piece = pieces[0]
    total_pieces = ngx * ngz
    spot = gx * ngz + piece

    def holder(index):
        block = lax.div(index, ngz)
        part = index - block * ngz
        return (block, gy, part + lax.rem(block, 2) * (ngz - 1 - 2 * part))

    x_low = holder(lax.rem(spot + (total_pieces - 1), total_pieces))
    x_high = holder(lax.rem(spot + 1, total_pieces))
    y_low = (gx, lax.rem(gy + (ngy - 1), ngy), gz)
    y_high = (gx, lax.rem(gy + 1, ngy), gz)
    peers = [(gx, gy, q) for q in gzs[1:]]
    chips = ngy // 2
    na, nb = ngx * 2, chips * ngz
    chip = lax.div(gy, 2)
    core = gy - 2 * chip
    same_core = [2 * c + core for c in around(chip, chips)]
    other_core = 2 * chip + 1 - core
    ma, mb = gx * 2 + core, chip * ngz + gz
    y_other = (gx, lax.rem(gy + ngy + 2 * core - 1, ngy), gz)

    def ring(offset, count):
        return min(offset, count - offset)

    steps_a = sorted(
        ((i, j) for i in range(ngx) for j in range(2) if i or j), key=lambda step: -ring(step[0], ngx)
    )
    steps_b = sorted(
        ((i, j) for i in range(chips) for j in range(ngz) if i or j),
        key=lambda step: -ring(step[0], chips) - ring(step[1], ngz),
    )
    group_a = [(gxs[i], other_core if j else gy, gz) for i, j in steps_a]
    group_b = [(gx, same_core[i], gzs[j]) for i, j in steps_b]

    here = pl.multiple_of(piece * ROWS, ROWS)
    my_rows = pl.ds(here, ROWS)
    loads = []
    for n, (src, dst) in enumerate(
        [
            (bed_in, bed),
            (vel_in, vel),
            (fric_in.at[my_rows, :], fric),
            (fstep_in.at[my_rows, :], fstep),
            (misfit_in.at[my_rows, :], misfit),
        ]
    ):
        copy = pltpu.make_async_copy(src, dst, load_sem.at[n])
        copy.start()
        loads.append(copy)

    barrier = pltpu.get_barrier_semaphore()
    far = [(-ring(i, ngx), device) for (i, _), device in zip(steps_a, group_a)]
    far += [(-ring(i, chips) - ring(j, ngz), device) for (i, j), device in zip(steps_b, group_b)]
    partners = [device for _, device in sorted(far, key=lambda item: item[0])] + [y_other]
    for partner in partners:
        pl.semaphore_signal(barrier, inc=1, device_id=partner, device_id_type=MESH)

    base = gz * depth
    for copy in loads:
        copy.wait()
    bedf = bed[...]
    vb0 = jnp.zeros(bedf.shape, F32)
    vb1 = jnp.zeros(bedf.shape, F32)
    for k in range(depth):
        at = bedf == base + k
        vb0 = jnp.where(at, vel[0, k], vb0)
        vb1 = jnp.where(at, vel[1, k], vb1)
    vbs[0] = vb0
    vbs[1] = vb1

    pl.semaphore_wait(barrier, len(partners))

    layers = pl.ds(base, depth)

    def moves(part, o):
        rows = pl.ds(pl.multiple_of(part * ROWS, ROWS), ROWS)
        return [
            (visc.at[:, rows, :], V.at[layers]),
            (binv.at[:, :, rows, :], B.at[:, layers]),
            (coup.at[:, rows, :], L.at[layers]),
            (vbs.at[:, rows, :], vbp.at[o]),
        ]

    locals_in = []
    for a, (src, dst) in enumerate(moves(piece, 0)):
        copy = pltpu.make_async_copy(src, dst, loc_sem.at[a])
        copy.start()
        locals_in.append(copy)
    incoming = [[], [], [], []]
    per_peer = [moves(pieces[o], o) for o in range(1, ngz)]
    for a in (3, 1, 2, 0):
        for o in (2, 1, 3):
            src, dst = per_peer[o - 1][a]
            copy = pltpu.make_async_remote_copy(
                src_ref=src, dst_ref=dst,
                send_sem=in_send.at[a, o], recv_sem=in_recv.at[a, o],
                device_id=peers[o - 1], device_id_type=MESH,
            )
            copy.start()
            incoming[a].append(copy)

    row = lax.broadcasted_iota(jnp.int32, (ROWS, LANES), 0)
    lane = lax.broadcasted_iota(jnp.int32, (ROWS, LANES), 1)
    column = jnp.zeros((ROWS, LANES), F32)
    for j in range(LANES // TILE):
        flag = ice[piece, j].astype(F32)
        column = jnp.where(lane // TILE == j, flag, column)
    has_ice = column > 0.5
    kbed = jnp.where(has_ice, bed[my_rows, :].astype(F32), NONE)
    friction = fric[...]
    load = misfit[...] * column

    for field in (Z0, ZA, S0, SA, ZB, SB):
        for c in range(2):
            field[c, 0] = jnp.zeros((ROWS, LANES), F32)
            field[c, NZ + 1] = jnp.zeros((ROWS, LANES), F32)
    V[NZ] = jnp.zeros((ROWS, LANES), F32)
    for ps in (ps0, ps3):
        ps[...] = jnp.zeros(ps.shape, F32)

    def pack_lane(packed, value, j):
        low, high = packed
        low = jnp.where(lane == j, pltpu.roll(value, j, 1), low)
        high = jnp.where(lane == j, pltpu.roll(value, (j + 1) % LANES, 1), high)
        return low, high

    def pack_rows(xs, value, j):
        xs[0, pl.ds(j, 1), :] = value[0:1, :]
        xs[1, pl.ds(j, 1), :] = value[ROWS - 1 : ROWS, :]

    def send_halo(index, xs, xr, ps, pr):
        copies = []
        for side, (src, dst, device) in enumerate(
            [
                (ps.at[0], pr.at[1], y_low),
                (ps.at[1], pr.at[0], y_high),
                (xs.at[0], xr.at[1], x_low),
                (xs.at[1], xr.at[0], x_high),
            ]
        ):
            copy = pltpu.make_async_remote_copy(
                src_ref=src, dst_ref=dst,
                send_sem=halo_send.at[index, side], recv_sem=halo_recv.at[index, side],
                device_id=device, device_id_type=MESH,
            )
            copy.start()
            copies.append(copy)
        return copies

    blank = jnp.zeros((ROWS, LANES), F32)
    for group, copy in zip(incoming[1:], locals_in[1:]):
        copy.wait()
        for remote in group:
            remote.wait_recv()
    speed0 = vbp[0, 0]
    speed1 = vbp[0, 1]
    for o in range(1, ngz):
        speed0 = speed0 + vbp[o, 0]
        speed1 = speed1 + vbp[o, 1]
    speed0 = jnp.where(has_ice, speed0, 0.0)
    speed1 = jnp.where(has_ice, speed1, 0.0)
    drive = friction * fstep[...]
    push0, push1 = drive * speed0, drive * speed1

    def apply_inverse(k, first, second):
        b0, b1, b2 = B[0, k], B[1, k], B[2, k]
        return b0 * first + b1 * second, b1 * first + b2 * second

    def rise(k, first, second, state, out):
        y0, y1, total = state
        link = L[k]
        t0 = first + link * y0
        t1 = second + link * y1
        y0, y1 = apply_inverse(k, t0, t1)
        out[0, k + 1] = y0
        out[1, k + 1] = y1
        return y0, y1, total + (t0 * y0 + t1 * y1)

    def first_rise(k, state):
        level = jnp.full((ROWS, LANES), k, jnp.int32).astype(F32)
        act = jnp.where(level >= kbed, 1.0, 0.0)
        beneath = jnp.where(level - 1.0 >= kbed, 1.0, 0.0)
        rest = 1.0 - act
        B[0, k] = act * B[0, k] + rest
        B[1, k] = act * B[1, k]
        B[2, k] = act * B[2, k] + rest
        L[k] = L[k] * act * beneath
        at = level == kbed
        first = jnp.where(at, push0, 0.0)
        second = jnp.where(at, push1, 0.0)
        return rise(k, first, second, state, Z0)

    state = blocked_loop(NZ, first_rise, (blank, blank, blank))
    rz0 = state[2]

    def fall(k, g0, g1, field):
        add0, add1 = apply_inverse(k, g0, g1)
        z0 = field[0, k + 1] + add0
        z1 = field[1, k + 1] + add1
        field[0, k + 1] = z0
        field[1, k + 1] = z1
        link = L[k]
        return z0, z1, link * z0, link * z1

    def fall_bare(k, g0, g1, field):
        z0, z1 = apply_inverse(k, g0, g1)
        field[0, k + 1] = z0
        field[1, k + 1] = z1
        link = L[k]
        return z0, z1, link * z0, link * z1

    seed_a0, seed_a1 = load * Z0[0, NZ], load * Z0[1, NZ]

    def fall_first(i, carry):
        k = NZ - 1 - i
        g0, g1, a0, a1, low, high = carry
        z0, z1, g0, g1 = fall(k, g0, g1, Z0)
        y0, y1, a0, a1 = fall_bare(k, a0, a1, ZA)
        packed = (low, high)
        for n, value in enumerate((z0, z1, y0, y1)):
            pack_rows(xs1, value, k + NZ * n)
            packed = pack_lane(packed, value, k + NZ * n)
        return (g0, g1, a0, a1) + packed

    carry = blocked_loop(NZ, fall_first, (blank, blank, seed_a0, seed_a1, blank, blank))
    ps1[0] = carry[4]
    ps1[1] = carry[5]
    halo1 = send_halo(1, xs1, xr1, ps1, pr1)
    raa = seed_a0 * ZA[0, NZ] + seed_a1 * ZA[1, NZ]

    locals_in[0].wait()
    for copy in incoming[0]:
        copy.wait_recv()

    def pack_viscosity(k, packed):
        value = V[k]
        pack_rows(xs0, value, k)
        return pack_lane(packed, value, k)

    packed = blocked_loop(NZ, pack_viscosity, (blank, blank))
    pack_rows(xs0, kbed, NZ)
    low, high = pack_lane(packed, kbed, NZ)
    ps0[0] = low
    ps0[1] = high
    halo0 = send_halo(0, xs0, xr0, ps0, pr0)

    def beside(value):
        east = pltpu.roll(value, ROWS - 1, 0)
        west = pltpu.roll(value, 1, 0)
        north = pltpu.roll(value, LANES - 1, 1)
        south = pltpu.roll(value, 1, 1)
        return east, west, north, south

    bed_e, bed_w, bed_n, bed_s = beside(kbed)
    bed_e = jnp.where(row == ROWS - 1, NONE, bed_e)
    bed_w = jnp.where(row == 0, NONE, bed_w)
    bed_n = jnp.where(lane == LANES - 1, NONE, bed_n)
    bed_s = jnp.where(lane == 0, NONE, bed_s)

    def layer_weights(k, down):
        level = jnp.full((ROWS, LANES), k, jnp.int32).astype(F32)
        value = V[k]
        act = jnp.where(level >= kbed, 1.0, 0.0)
        above = jnp.where((level + 1.0 >= kbed) & (level + 1.0 < NZ), 1.0, 0.0)
        bedflag = jnp.where(level == kbed, 1.0, 0.0)
        east, west, north, south = beside(value)
        half_act = 0.5 * act
        up = (VERTICAL * (value + V[k + 1])) * (half_act * above)
        we = (value + east) * jnp.where(level >= bed_e, half_act, 0.0)
        ww = (value + west) * jnp.where(level >= bed_w, half_act, 0.0)
        wn = (value + north) * jnp.where(level >= bed_n, half_act, 0.0)
        ws = (value + south) * jnp.where(level >= bed_s, half_act, 0.0)
        WU[k + 1] = up
        WE[k] = we
        WW[k] = ww
        WN[k] = wn
        WS[k] = ws
        ew, ns = we + ww, wn + ws
        rest = (up + down) + friction * bedflag + (1.0 - act)
        D0[k] = STRETCH * ew + ns + rest
        D1[k] = ew + STRETCH * ns + rest
        return up

    WU[0] = blank
    blocked_loop(NZ, layer_weights, blank)

    def operate(k, weights, field):
        up, down, we, ww, wn, ws, d0, d1 = weights
        result = []
        for c in range(2):
            value = field[c, k + 1]
            east, west, north, south = beside(value)
            vertical = up * field[c, k + 2] + down * field[c, k]
            ew = we * east + ww * west
            ns = wn * north + ws * south
            if c == 0:
                result.append(d0 * value - vertical - STRETCH * ew - ns)
            else:
                result.append(d1 * value - vertical - ew - STRETCH * ns)
        return result

    def keep(k, weights, field, out):
        image = operate(k, weights, field)
        out[0, k + 1] = image[0]
        out[1, k + 1] = image[1]

    def complete(k, inner, xr, low, high, n, lanes_from):
        return [
            inner[c, k + 1] + shared(xr, NZ * (n + c) + k, low, high, lanes_from + NZ * c + k)
            for c in range(2)
        ]

    def weights_of(k):
        return WU[k + 1], WU[k], WE[k], WW[k], WN[k], WS[k], D0[k], D1[k]

    def against(field, k, image, total):
        return total + (field[0, k + 1] * image[0] + field[1, k + 1] * image[1])

    def inner_first(k, carry):
        weights = weights_of(k)
        keep(k, weights, Z0, S0)
        keep(k, weights, ZA, SA)
        return carry

    blocked_loop(NZ, inner_first, 0)
    for copy in halo0:
        copy.wait_recv()
    rows_level = lax.broadcasted_iota(jnp.int32, (NZ, LANES), 0).astype(F32)
    lanes_level = lane.astype(F32)
    x_edges = (spot == 0, spot == total_pieces - 1)
    y_edges = (gy == 0, gy == ngy - 1)
    FY = []
    for side in range(2):
        own_bed = xs0[side, NZ : NZ + 1, :]
        their_bed = jnp.where(x_edges[side], NONE, xr0[side, NZ : NZ + 1, :])
        both = (rows_level >= own_bed) & (rows_level >= their_bed)
        face = jnp.where(both, 0.5 * (xs0[side, :NZ, :] + xr0[side, :NZ, :]), 0.0)
        FX[side, :NZ, :] = STRETCH * face
        FX[side, NZ:, :] = face
        own, theirs = ps0[side], pr0[side]
        own_bed = jnp.sum(jnp.where(lane == NZ, own, 0.0), axis=1, keepdims=True)
        their_bed = jnp.sum(jnp.where(lane == NZ, theirs, 0.0), axis=1, keepdims=True)
        their_bed = jnp.where(y_edges[side], NONE, their_bed)
        both = (lanes_level >= own_bed) & (lanes_level >= their_bed) & (lane < NZ)
        face = jnp.where(both, 0.5 * (own + theirs), 0.0)
        face = face + STRETCH * pltpu.roll(face, NZ, 1)
        FY.append(face + pltpu.roll(face, 2 * NZ, 1))

    def exchange(xs, xr, ps, pr, fields, packs):
        for side in range(2):
            for n in range(fields):
                part = pl.ds(2 * NZ * n, 2 * NZ)
                xr[side, part, :] = FX[side] * (xs[side, part, :] - xr[side, part, :])
            for n in range(packs):
                part = pl.ds(ROWS * n, ROWS)
                pr[side, part, :] = FY[side] * (ps[side, part, :] - pr[side, part, :])

    def shared(xr, xj, low, high, lj):
        result = jnp.where(row == 0, xr[0, pl.ds(xj, 1), :], 0.0)
        result = jnp.where(row == ROWS - 1, xr[1, pl.ds(xj, 1), :], result)
        result = result + jnp.where(lane == 0, pltpu.roll(low, lax.rem(LANES - lj, LANES), 1), 0.0)
        return result + jnp.where(lane == LANES - 1, pltpu.roll(high, LANES - 1 - lj, 1), 0.0)

    def shared_energy(xs, ps, first, pack, start, xr, pr, xr_first, pr_pack, pr_start):
        total = blank
        for side in range(2):
            for n in range(2 * NZ // ROWS):
                mine = xs[side, pl.ds(2 * NZ * first + ROWS * n, ROWS), :]
                total = total + mine * xr[side, pl.ds(2 * NZ * xr_first + ROWS * n, ROWS), :]
            mine = ps[side, pl.ds(ROWS * pack, ROWS), :]
            theirs = pr[side, pl.ds(ROWS * pr_pack, ROWS), :]
            if start != pr_start:
                mine = pltpu.roll(mine, (pr_start - start) % LANES, 1)
            inside = (lane >= pr_start) & (lane < pr_start + 2 * NZ)
            total = total + jnp.where(inside, mine * theirs, 0.0)
        return total

    for copy in halo1:
        copy.wait_recv()
    exchange(xs1, xr1, ps1, pr1, 2, 1)
    low1, high1 = pr1[0], pr1[1]

    def middle_rise(k, carry):
        pq0, paa, main, extra = carry
        w = complete(k, S0, xr1, low1, high1, 0, 0)
        wa = complete(k, SA, xr1, low1, high1, 2, 2 * NZ)
        pq0 = against(Z0, k, w, pq0)
        paa = against(ZA, k, wa, paa)
        main = rise(k, w[0], w[1], main, S0)
        extra = rise(k, wa[0], wa[1], extra, SA)
        return pq0, paa, main, extra

    triple = (blank, blank, blank)
    pq0, paa, main, extra = blocked_loop(NZ, middle_rise, (blank, blank, triple, triple))
    g0, gaa = main[2], extra[2]
    seed_b0, seed_b1 = load * S0[0, NZ], load * S0[1, NZ]

    def fall_second(i, carry):
        k = NZ - 1 - i
        g0, g1, h0, h1, b0, b1, low1, high1, low2, high2 = carry
        z0, z1, g0, g1 = fall(k, g0, g1, S0)
        a0, a1, h0, h1 = fall(k, h0, h1, SA)
        y0, y1, b0, b1 = fall_bare(k, b0, b1, ZB)
        packed = (low1, high1)
        for n, value in enumerate((y0, y1, z0, z1)):
            pack_rows(xs2, value, k + NZ * n)
            packed = pack_lane(packed, value, k + NZ * n)
        other = (low2, high2)
        for n, value in enumerate((a0, a1)):
            pack_rows(xs2, value, k + NZ * (n + 4))
            other = pack_lane(other, value, k + NZ * n)
        return (g0, g1, h0, h1, b0, b1) + packed + other

    carry = blocked_loop(
        NZ, fall_second, (blank, blank, blank, blank, seed_b0, seed_b1, blank, blank, blank, blank)
    )
    for n in range(2):
        ps2[0, ROWS * n : ROWS * (n + 1), :] = carry[6 + 2 * n]
        ps2[1, ROWS * n : ROWS * (n + 1), :] = carry[7 + 2 * n]
    halo2 = send_halo(2, xs2, xr2, ps2, pr2)
    rab = seed_a0 * ZB[0, NZ] + seed_a1 * ZB[1, NZ]
    rbb = seed_b0 * ZB[0, NZ] + seed_b1 * ZB[1, NZ]

    def inner_second(k, carry):
        d0, daa = carry
        weights = weights_of(k)
        keep(k, weights, ZB, SB)
        d0 = against(S0, k, operate(k, weights, S0), d0)
        daa = against(SA, k, operate(k, weights, SA), daa)
        return d0, daa

    d0, daa = blocked_loop(NZ, inner_second, (blank, blank))
    for copy in halo2:
        copy.wait_recv()
    exchange(xs2, xr2, ps2, pr2, 3, 2)
    low2, high2 = pr2[0, :ROWS, :], pr2[1, :ROWS, :]

    def last_rise(k, carry):
        pab, pbb, gab, main = carry
        w = complete(k, SB, xr2, low2, high2, 0, 0)
        pab = against(ZA, k, w, pab)
        pbb = against(ZB, k, w, pbb)
        gab = against(SA, k, w, gab)
        main = rise(k, w[0], w[1], main, SB)
        return pab, pbb, gab, main

    pab, pbb, gab, main = blocked_loop(NZ, last_rise, (blank, blank, blank, triple))
    gbb = main[2]

    def fall_third(i, carry):
        k = NZ - 1 - i
        g0, g1, low, high = carry
        z0, z1, g0, g1 = fall(k, g0, g1, SB)
        packed = (low, high)
        for n, value in enumerate((z0, z1)):
            pack_rows(xs3, value, k + NZ * n)
            packed = pack_lane(packed, value, k + NZ * n)
        return (g0, g1) + packed

    carry = blocked_loop(NZ, fall_third, (blank, blank, blank, blank))
    ps3[0] = carry[2]
    ps3[1] = carry[3]
    halo3 = send_halo(3, xs3, xr3, ps3, pr3)

    finals = []
    rest = []
    places = [
        gathered.at[0, :, :, my_rows, :],
        gathered.at[1, :, :, my_rows, :],
        adj.at[:, :, my_rows, :],
        hess.at[my_rows, :],
    ]

    def give_back(n, field):
        for o in range(1, ngz):
            send_back(n, o, field.at[:, pl.ds(1 + gzs[o] * depth, depth)])
        copy = pltpu.make_async_copy(field.at[:, pl.ds(1 + base, depth)], places[n], loc_sem.at[n])
        copy.start()
        finals.append(copy)

    def send_back(n, o, src):
        copy = pltpu.make_async_remote_copy(
            src_ref=src, dst_ref=places[n],
            send_sem=out_send.at[n, o], recv_sem=out_recv.at[n, o],
            device_id=peers[o - 1], device_id_type=MESH,
        )
        copy.start()
        rest.append(copy)

    give_back(0, Z0)
    give_back(1, S0)
    d0 = d0 + shared_energy(xs2, ps2, 1, 0, 2 * NZ, xr2, pr2, 1, 0, 2 * NZ)
    daa = daa + shared_energy(xs2, ps2, 2, 1, 0, xr2, pr2, 2, 1, 0)

    stages = ((group_a, ra, red_recv_a, ma), (group_b, rb, red_recv_b, mb))

    def gather_sums(values):
        for n, value in enumerate(values):
            stack[n : n + 1, :] = jnp.sum(value, axis=0, keepdims=True)
        each = jnp.sum(stack[...], axis=1, keepdims=True)
        return jnp.sum(jnp.where(lane == row, each, 0.0), axis=0, keepdims=True)

    def send_sum(stage, value):
        rt[stage] = value
        group, received, sem, place = stages[stage]
        received[place] = value
        copies = []
        for o, device in enumerate(group):
            copy = pltpu.make_async_remote_copy(
                src_ref=rt.at[stage], dst_ref=received.at[place],
                send_sem=red_send.at[stage, o], recv_sem=sem.at[o],
                device_id=device, device_id_type=MESH,
            )
            copy.start()
            copies.append(copy)
        return copies

    def finish_sum(stage, copies):
        for copy in copies:
            copy.wait_recv()
        return jnp.sum(stages[stage][1][...], axis=0)

    def spread(total, count):
        each = jnp.sum(jnp.where(lane == row, total, 0.0), axis=1, keepdims=True)
        each = jnp.broadcast_to(each, (ROWS, LANES))
        return [each[n : n + 1, :] for n in range(count)]


    def inner_third(k, carry):
        dab, dbb = carry
        image = operate(k, weights_of(k), SB)
        return against(SA, k, image, dab), against(SB, k, image, dbb)

    dab, dbb = blocked_loop(NZ, inner_third, (blank, blank))
    for copy in halo3:
        copy.wait_recv()
    exchange(xs3, xr3, ps3, pr3, 1, 1)
    dab = dab + shared_energy(xs2, ps2, 2, 1, 0, xr3, pr3, 0, 0, 0)
    dbb = dbb + shared_energy(xs3, ps3, 0, 0, 0, xr3, pr3, 0, 0, 0)
    sums = [rz0, pq0, g0, d0, raa, rab, rbb, paa, pab, pbb, gaa, gab, gbb, daa, dab, dbb]
    first = send_sum(0, gather_sums(sums))
    second = send_sum(1, finish_sum(0, first))
    reductions = first + second
    (rz0, pq0, g0, d0, raa, rab, rbb, paa, pab, pbb, gaa, gab, gbb, daa, dab, dbb) = spread(finish_sum(1, second), 16)

    def combination(rz, pq, g, d):
        step = rz / pq
        renewed = step * step * g - rz
        grow = 1.0 + renewed / rz
        energy = grow * grow * pq - 2.0 * grow * step * g + step * step * d
        second = renewed / energy
        return step + second * grow, -(second * step)

    c0, c1 = combination(rz0, pq0, g0, d0)

    def form(aa, ab, bb):
        return c0 * c0 * aa + 2.0 * (c0 * c1) * ab + c1 * c1 * bb

    e0, e1 = combination(form(raa, rab, rbb), form(paa, pab, pbb), form(gaa, gab, gbb), form(daa, dab, dbb))
    f_za, f_zb, f_sa, f_sb = e0 * c0, e0 * c1, e1 * c0, e1 * c1

    def adjoints(k, carry):
        level = jnp.full((ROWS, LANES), k, jnp.int32).astype(F32)
        at = level == kbed
        out = []
        for c in range(2):
            value = (f_za * ZA[c, k + 1] + f_zb * ZB[c, k + 1]) + (f_sa * SA[c, k + 1] + f_sb * SB[c, k + 1])
            ZA[c, k + 1] = value
            out.append(jnp.where(at, value, carry[c]))
        return tuple(out)

    landed = len(rest)
    basal = blocked_loop(NZ, adjoints, (blank, blank))
    give_back(2, ZA)
    action = friction * (speed0 * basal[0] + speed1 * basal[1])
    hess[my_rows, :] = action
    vbs[0, my_rows, :] = action
    for o in range(1, ngz):
        send_back(3, o, vbs.at[0, my_rows, :])
    for copy in finals[:2]:
        copy.wait()
    for copy in rest[:landed]:
        copy.wait_recv()

    def increments(k, carry):
        for c in range(2):
            gathered[0, c, k] = c0 * gathered[0, c, k] + c1 * gathered[1, c, k]
        return carry

    lax.fori_loop(0, depth, increments, 0)
    final = pltpu.make_async_copy(gathered.at[0], inc, loc_sem.at[3])
    final.start()

    for copy in finals[2:] + [final]:
        copy.wait()
    for copy in rest[landed:]:
        copy.wait_recv()
    for copy in rest:
        copy.wait_send()
    for group in incoming:
        for copy in group:
            copy.wait_send()
    for copy in halo0 + halo1 + halo2 + halo3 + reductions:
        copy.wait_send()


def deliver(inc_in, adj_in, hess_in, inc, adj, hess, first, second, third, sem):
    held = [(inc_in.at[c], first.at[c], inc.at[c]) for c in range(2)]
    held += [(adj_in.at[c], second.at[c], adj.at[c]) for c in range(2)]
    held += [(hess_in, third, hess)]
    reads = [pltpu.make_async_copy(src, mid, sem.at[n, 0]) for n, (src, mid, _) in enumerate(held)]
    writes = [pltpu.make_async_copy(mid, dst, sem.at[n, 1]) for n, (_, mid, dst) in enumerate(held)]
    for copy in reads:
        copy.start()
    for read, write in zip(reads, writes):
        read.wait()
        write.start()
    for copy in writes:
        copy.wait()


def local(sizes, *args):
    ngx, ngy, ngz = sizes
    field = pltpu.VMEM((NZ, ROWS, LANES), F32)
    state = pltpu.VMEM((2, NZ + 2, ROWS, LANES), F32)
    depth, rows, lanes = args[1].shape
    dma = pltpu.SemaphoreType.DMA

    def halo(length, packs):
        return [pltpu.VMEM((2, length, LANES), F32)] * 2 + [pltpu.VMEM((2, packs * ROWS, LANES), F32)] * 2

    na, nb = ngx * 2, (ngy // 2) * ngz
    scratch = (
        [pltpu.VMEM((2, depth, rows, lanes), F32), pltpu.VMEM((rows, lanes), jnp.int32)]
        + [pltpu.VMEM((ROWS, LANES), F32)] * 3
        + [pltpu.VMEM((2, 2 * NZ, LANES), F32)]
        + [pltpu.VMEM((NZ + 1, ROWS, LANES), F32), pltpu.VMEM((3, NZ, ROWS, LANES), F32), field]
        + [pltpu.VMEM((2, rows, lanes), F32), pltpu.VMEM((ngz, 2, ROWS, LANES), F32)]
        + [pltpu.VMEM((NZ + 1, ROWS, LANES), F32)]
        + [field] * 6
        + [state] * 6
        + halo(NZ + 8, 1) + halo(4 * NZ, 1) + halo(6 * NZ, 2) + halo(2 * NZ, 1)
        + [pltpu.VMEM((ROWS, LANES), F32), pltpu.VMEM((2, 1, LANES), F32)]
        + [pltpu.VMEM((na, 1, LANES), F32), pltpu.VMEM((nb, 1, LANES), F32)]
        + [pltpu.VMEM((2, 2, depth, rows, lanes), F32)]
        + [dma((5,)), dma((4,)), dma((4, ngz)), dma((4, ngz)), dma((4, 4)), dma((4, 4))]
        + [dma((2, max(na, nb))), dma((na,)), dma((nb,)), dma((4, ngz)), dma((4, ngz))]
    )
    vmem = pl.BlockSpec(memory_space=pltpu.VMEM)
    hbm = pl.BlockSpec(memory_space=pl.ANY)
    smem = pl.BlockSpec(memory_space=pltpu.SMEM)
    shapes = (
        jax.ShapeDtypeStruct((2, depth, rows, lanes), F32),
        jax.ShapeDtypeStruct((2, depth, rows, lanes), F32),
        jax.ShapeDtypeStruct((rows, lanes), F32),
    )
    results = pl.pallas_call(
        functools.partial(kernel, sizes),
        out_shape=shapes,
        in_specs=[hbm] * 7 + [smem, hbm],
        out_specs=(hbm, hbm, vmem),
        scratch_shapes=scratch,
        compiler_params=pltpu.CompilerParams(
            collective_id=0, has_side_effects=True, vmem_limit_bytes=62 * 1024 * 1024
        ),
    )(*args)
    return pl.pallas_call(
        deliver,
        out_shape=shapes,
        in_specs=[hbm] * 3,
        out_specs=(hbm, hbm, hbm),
        scratch_shapes=[pltpu.VMEM(shape.shape, F32) for shape in shapes] + [dma((5, 2))],
        compiler_params=pltpu.CompilerParams(vmem_limit_bytes=62 * 1024 * 1024),
    )(*results)


def solution(mesh):
    sizes = (mesh.shape["gx"], mesh.shape["gy"], mesh.shape["gz"])
    wide, cell, flat = P(None, "gz", "gx", "gy"), P("gz", "gx", "gy"), P("gx", "gy")
    return jax.shard_map(
        functools.partial(local, sizes),
        mesh=mesh,
        in_specs=(wide, cell, wide, cell, flat, flat, flat, flat, flat),
        out_specs=(wide, wide, flat),
        check_vma=False,
    )
```

```python
import functools

import jax
import jax.numpy as jnp
from jax import lax
from jax.experimental import pallas as pl
from jax.experimental.pallas import tpu as pltpu
from jax.sharding import PartitionSpec as P

TILE = 16
VERTICAL = 8.0
STRETCH = 4.0
NONE = 1000.0
MESH = pl.DeviceIdType.MESH
F32 = jnp.float32
NZ = 32
ROWS = 16
LANES = 128
UNROLL = 32


def blocked_loop(steps, body, carry):
    def chunk(index, state):
        for inner in range(UNROLL):
            state = body(index * UNROLL + inner, state)
        return state

    return lax.fori_loop(0, steps // UNROLL, chunk, carry)


def kernel(
    sizes,
    vel_in, visc, binv, coup, fric_in, fstep_in, misfit_in, ice, bed_in,
    inc, adj, hess,
    vel, bed, fric, fstep, misfit,
    FX, V, B, L, vbs, vbp, WU, WE, WW, WN, WS, D0, D1,
    Z0, ZA, S0, SA, ZB, SB,
    xs0, xr0, ps0, pr0, xs1, xr1, ps1, pr1, xs2, xr2, ps2, pr2, xs3, xr3, ps3, pr3,
    stack, rt, ra, rb,
    gathered, load_sem, loc_sem, in_send, in_recv, halo_send, halo_recv, red_send, red_recv_a, red_recv_b,
    out_send, out_recv,
):
    ngx, ngy, ngz = sizes
    gx, gy, gz = lax.axis_index("gx"), lax.axis_index("gy"), lax.axis_index("gz")
    depth = NZ // ngz
    odd = lax.rem(gx, 2)

    def around(index, count):
        return [index] + [lax.rem(index + o, count) for o in range(1, count)]

    def piece_of(q):
        return q + odd * (ngz - 1 - 2 * q)

    gxs, gzs = around(gx, ngx), around(gz, ngz)
    pieces = [piece_of(q) for q in gzs]
    piece = pieces[0]
    total_pieces = ngx * ngz
    spot = gx * ngz + piece

    def holder(index):
        block = lax.div(index, ngz)
        part = index - block * ngz
        return (block, gy, part + lax.rem(block, 2) * (ngz - 1 - 2 * part))

    x_low = holder(lax.rem(spot + (total_pieces - 1), total_pieces))
    x_high = holder(lax.rem(spot + 1, total_pieces))
    y_low = (gx, lax.rem(gy + (ngy - 1), ngy), gz)
    y_high = (gx, lax.rem(gy + 1, ngy), gz)
    peers = [(gx, gy, q) for q in gzs[1:]]
    chips = ngy // 2
    na, nb = ngx * 2, chips * ngz
    chip = lax.div(gy, 2)
    core = gy - 2 * chip
    same_core = [2 * c + core for c in around(chip, chips)]
    other_core = 2 * chip + 1 - core
    ma, mb = gx * 2 + core, chip * ngz + gz
    y_other = (gx, lax.rem(gy + ngy + 2 * core - 1, ngy), gz)

    def ring(offset, count):
        return min(offset, count - offset)

    steps_a = sorted(
        ((i, j) for i in range(ngx) for j in range(2) if i or j), key=lambda step: -ring(step[0], ngx)
    )
    steps_b = sorted(
        ((i, j) for i in range(chips) for j in range(ngz) if i or j),
        key=lambda step: -ring(step[0], chips) - ring(step[1], ngz),
    )
    group_a = [(gxs[i], other_core if j else gy, gz) for i, j in steps_a]
    group_b = [(gx, same_core[i], gzs[j]) for i, j in steps_b]

    here = pl.multiple_of(piece * ROWS, ROWS)
    my_rows = pl.ds(here, ROWS)
    loads = []
    for n, (src, dst) in enumerate(
        [
            (bed_in, bed),
            (vel_in, vel),
            (fric_in.at[my_rows, :], fric),
            (fstep_in.at[my_rows, :], fstep),
            (misfit_in.at[my_rows, :], misfit),
        ]
    ):
        copy = pltpu.make_async_copy(src, dst, load_sem.at[n])
        copy.start()
        loads.append(copy)

    barrier = pltpu.get_barrier_semaphore()
    far = [(-ring(i, ngx), device) for (i, _), device in zip(steps_a, group_a)]
    far += [(-ring(i, chips) - ring(j, ngz), device) for (i, j), device in zip(steps_b, group_b)]
    partners = [device for _, device in sorted(far, key=lambda item: item[0])] + [y_other]
    for partner in partners:
        pl.semaphore_signal(barrier, inc=1, device_id=partner, device_id_type=MESH)

    base = gz * depth
    for copy in loads:
        copy.wait()
    bedf = bed[...]
    vb0 = jnp.zeros(bedf.shape, F32)
    vb1 = jnp.zeros(bedf.shape, F32)
    for k in range(depth):
        at = bedf == base + k
        vb0 = jnp.where(at, vel[0, k], vb0)
        vb1 = jnp.where(at, vel[1, k], vb1)
    vbs[0] = vb0
    vbs[1] = vb1

    pl.semaphore_wait(barrier, len(partners))

    layers = pl.ds(base, depth)

    def moves(part, o):
        rows = pl.ds(pl.multiple_of(part * ROWS, ROWS), ROWS)
        return [
            (visc.at[:, rows, :], V.at[layers]),
            (binv.at[:, :, rows, :], B.at[:, layers]),
            (coup.at[:, rows, :], L.at[layers]),
            (vbs.at[:, rows, :], vbp.at[o]),
        ]

    locals_in = []
    for a, (src, dst) in enumerate(moves(piece, 0)):
        copy = pltpu.make_async_copy(src, dst, loc_sem.at[a])
        copy.start()
        locals_in.append(copy)
    incoming = [[], [], [], []]
    per_peer = [moves(pieces[o], o) for o in range(1, ngz)]
    for a in (3, 1, 2, 0):
        for o in (2, 1, 3):
            src, dst = per_peer[o - 1][a]
            copy = pltpu.make_async_remote_copy(
                src_ref=src, dst_ref=dst,
                send_sem=in_send.at[a, o], recv_sem=in_recv.at[a, o],
                device_id=peers[o - 1], device_id_type=MESH,
            )
            copy.start()
            incoming[a].append(copy)

    row = lax.broadcasted_iota(jnp.int32, (ROWS, LANES), 0)
    lane = lax.broadcasted_iota(jnp.int32, (ROWS, LANES), 1)
    column = jnp.zeros((ROWS, LANES), F32)
    for j in range(LANES // TILE):
        flag = ice[piece, j].astype(F32)
        column = jnp.where(lane // TILE == j, flag, column)
    has_ice = column > 0.5
    kbed = jnp.where(has_ice, bed[my_rows, :].astype(F32), NONE)
    friction = fric[...]
    load = misfit[...] * column

    for field in (Z0, ZA, S0, SA, ZB, SB):
        for c in range(2):
            field[c, 0] = jnp.zeros((ROWS, LANES), F32)
            field[c, NZ + 1] = jnp.zeros((ROWS, LANES), F32)
    V[NZ] = jnp.zeros((ROWS, LANES), F32)
    for ps in (ps0, ps3):
        ps[...] = jnp.zeros(ps.shape, F32)

    def pack_lane(packed, value, j):
        low, high = packed
        low = jnp.where(lane == j, pltpu.roll(value, j, 1), low)
        high = jnp.where(lane == j, pltpu.roll(value, (j + 1) % LANES, 1), high)
        return low, high

    def pack_rows(xs, value, j):
        xs[0, pl.ds(j, 1), :] = value[0:1, :]
        xs[1, pl.ds(j, 1), :] = value[ROWS - 1 : ROWS, :]

    def send_halo(index, xs, xr, ps, pr):
        copies = []
        for side, (src, dst, device) in enumerate(
            [
                (ps.at[0], pr.at[1], y_low),
                (ps.at[1], pr.at[0], y_high),
                (xs.at[0], xr.at[1], x_low),
                (xs.at[1], xr.at[0], x_high),
            ]
        ):
            copy = pltpu.make_async_remote_copy(
                src_ref=src, dst_ref=dst,
                send_sem=halo_send.at[index, side], recv_sem=halo_recv.at[index, side],
                device_id=device, device_id_type=MESH,
            )
            copy.start()
            copies.append(copy)
        return copies

    blank = jnp.zeros((ROWS, LANES), F32)
    for group, copy in zip(incoming[1:], locals_in[1:]):
        copy.wait()
        for remote in group:
            remote.wait_recv()
    speed0 = vbp[0, 0]
    speed1 = vbp[0, 1]
    for o in range(1, ngz):
        speed0 = speed0 + vbp[o, 0]
        speed1 = speed1 + vbp[o, 1]
    speed0 = jnp.where(has_ice, speed0, 0.0)
    speed1 = jnp.where(has_ice, speed1, 0.0)
    drive = friction * fstep[...]
    push0, push1 = drive * speed0, drive * speed1

    def apply_inverse(k, first, second):
        b0, b1, b2 = B[0, k], B[1, k], B[2, k]
        return b0 * first + b1 * second, b1 * first + b2 * second

    def rise(k, first, second, state, out):
        y0, y1, total = state
        link = L[k]
        t0 = first + link * y0
        t1 = second + link * y1
        y0, y1 = apply_inverse(k, t0, t1)
        out[0, k + 1] = y0
        out[1, k + 1] = y1
        return y0, y1, total + (t0 * y0 + t1 * y1)

    def first_rise(k, state):
        level = jnp.full((ROWS, LANES), k, jnp.int32).astype(F32)
        act = jnp.where(level >= kbed, 1.0, 0.0)
        beneath = jnp.where(level - 1.0 >= kbed, 1.0, 0.0)
        rest = 1.0 - act
        B[0, k] = act * B[0, k] + rest
        B[1, k] = act * B[1, k]
        B[2, k] = act * B[2, k] + rest
        L[k] = L[k] * act * beneath
        at = level == kbed
        first = jnp.where(at, push0, 0.0)
        second = jnp.where(at, push1, 0.0)
        return rise(k, first, second, state, Z0)

    state = blocked_loop(NZ, first_rise, (blank, blank, blank))
    rz0 = state[2]

    def fall(k, g0, g1, field):
        add0, add1 = apply_inverse(k, g0, g1)
        z0 = field[0, k + 1] + add0
        z1 = field[1, k + 1] + add1
        field[0, k + 1] = z0
        field[1, k + 1] = z1
        link = L[k]
        return z0, z1, link * z0, link * z1

    def fall_bare(k, g0, g1, field):
        z0, z1 = apply_inverse(k, g0, g1)
        field[0, k + 1] = z0
        field[1, k + 1] = z1
        link = L[k]
        return z0, z1, link * z0, link * z1

    seed_a0, seed_a1 = load * Z0[0, NZ], load * Z0[1, NZ]

    def fall_first(i, carry):
        k = NZ - 1 - i
        g0, g1, a0, a1, low, high = carry
        z0, z1, g0, g1 = fall(k, g0, g1, Z0)
        y0, y1, a0, a1 = fall_bare(k, a0, a1, ZA)
        packed = (low, high)
        for n, value in enumerate((z0, z1, y0, y1)):
            pack_rows(xs1, value, k + NZ * n)
            packed = pack_lane(packed, value, k + NZ * n)
        return (g0, g1, a0, a1) + packed

    carry = blocked_loop(NZ, fall_first, (blank, blank, seed_a0, seed_a1, blank, blank))
    ps1[0] = carry[4]
    ps1[1] = carry[5]
    halo1 = send_halo(1, xs1, xr1, ps1, pr1)
    raa = seed_a0 * ZA[0, NZ] + seed_a1 * ZA[1, NZ]

    locals_in[0].wait()
    for copy in incoming[0]:
        copy.wait_recv()

    def pack_viscosity(k, packed):
        value = V[k]
        pack_rows(xs0, value, k)
        return pack_lane(packed, value, k)

    packed = blocked_loop(NZ, pack_viscosity, (blank, blank))
    pack_rows(xs0, kbed, NZ)
    low, high = pack_lane(packed, kbed, NZ)
    ps0[0] = low
    ps0[1] = high
    halo0 = send_halo(0, xs0, xr0, ps0, pr0)

    def beside(value):
        east = pltpu.roll(value, ROWS - 1, 0)
        west = pltpu.roll(value, 1, 0)
        north = pltpu.roll(value, LANES - 1, 1)
        south = pltpu.roll(value, 1, 1)
        return east, west, north, south

    bed_e, bed_w, bed_n, bed_s = beside(kbed)
    bed_e = jnp.where(row == ROWS - 1, NONE, bed_e)
    bed_w = jnp.where(row == 0, NONE, bed_w)
    bed_n = jnp.where(lane == LANES - 1, NONE, bed_n)
    bed_s = jnp.where(lane == 0, NONE, bed_s)

    def layer_weights(k, down):
        level = jnp.full((ROWS, LANES), k, jnp.int32).astype(F32)
        value = V[k]
        act = jnp.where(level >= kbed, 1.0, 0.0)
        above = jnp.where((level + 1.0 >= kbed) & (level + 1.0 < NZ), 1.0, 0.0)
        bedflag = jnp.where(level == kbed, 1.0, 0.0)
        east, west, north, south = beside(value)
        half_act = 0.5 * act
        up = (VERTICAL * (value + V[k + 1])) * (half_act * above)
        we = (value + east) * jnp.where(level >= bed_e, half_act, 0.0)
        ww = (value + west) * jnp.where(level >= bed_w, half_act, 0.0)
        wn = (value + north) * jnp.where(level >= bed_n, half_act, 0.0)
        ws = (value + south) * jnp.where(level >= bed_s, half_act, 0.0)
        WU[k + 1] = up
        WE[k] = we
        WW[k] = ww
        WN[k] = wn
        WS[k] = ws
        ew, ns = we + ww, wn + ws
        rest = (up + down) + friction * bedflag + (1.0 - act)
        D0[k] = STRETCH * ew + ns + rest
        D1[k] = ew + STRETCH * ns + rest
        return up

    WU[0] = blank
    blocked_loop(NZ, layer_weights, blank)

    def operate(k, weights, field):
        up, down, we, ww, wn, ws, d0, d1 = weights
        result = []
        for c in range(2):
            value = field[c, k + 1]
            east, west, north, south = beside(value)
            vertical = up * field[c, k + 2] + down * field[c, k]
            ew = we * east + ww * west
            ns = wn * north + ws * south
            if c == 0:
                result.append(d0 * value - vertical - STRETCH * ew - ns)
            else:
                result.append(d1 * value - vertical - ew - STRETCH * ns)
        return result

    def keep(k, weights, field, out):
        image = operate(k, weights, field)
        out[0, k + 1] = image[0]
        out[1, k + 1] = image[1]

    def complete(k, inner, xr, low, high, n, lanes_from):
        return [
            inner[c, k + 1] + shared(xr, NZ * (n + c) + k, low, high, lanes_from + NZ * c + k)
            for c in range(2)
        ]

    def weights_of(k):
        return WU[k + 1], WU[k], WE[k], WW[k], WN[k], WS[k], D0[k], D1[k]

    def against(field, k, image, total):
        return total + (field[0, k + 1] * image[0] + field[1, k + 1] * image[1])

    def inner_first(k, carry):
        weights = weights_of(k)
        keep(k, weights, Z0, S0)
        keep(k, weights, ZA, SA)
        return carry

    blocked_loop(NZ, inner_first, 0)
    for copy in halo0:
        copy.wait_recv()
    rows_level = lax.broadcasted_iota(jnp.int32, (NZ, LANES), 0).astype(F32)
    lanes_level = lane.astype(F32)
    x_edges = (spot == 0, spot == total_pieces - 1)
    y_edges = (gy == 0, gy == ngy - 1)
    FY = []
    for side in range(2):
        own_bed = xs0[side, NZ : NZ + 1, :]
        their_bed = jnp.where(x_edges[side], NONE, xr0[side, NZ : NZ + 1, :])
        both = (rows_level >= own_bed) & (rows_level >= their_bed)
        face = jnp.where(both, 0.5 * (xs0[side, :NZ, :] + xr0[side, :NZ, :]), 0.0)
        FX[side, :NZ, :] = STRETCH * face
        FX[side, NZ:, :] = face
        own, theirs = ps0[side], pr0[side]
        own_bed = jnp.sum(jnp.where(lane == NZ, own, 0.0), axis=1, keepdims=True)
        their_bed = jnp.sum(jnp.where(lane == NZ, theirs, 0.0), axis=1, keepdims=True)
        their_bed = jnp.where(y_edges[side], NONE, their_bed)
        both = (lanes_level >= own_bed) & (lanes_level >= their_bed) & (lane < NZ)
        face = jnp.where(both, 0.5 * (own + theirs), 0.0)
        face = face + STRETCH * pltpu.roll(face, NZ, 1)
        FY.append(face + pltpu.roll(face, 2 * NZ, 1))

    def exchange(xs, xr, ps, pr, fields, packs):
        for side in range(2):
            for n in range(fields):
                part = pl.ds(2 * NZ * n, 2 * NZ)
                xr[side, part, :] = FX[side] * (xs[side, part, :] - xr[side, part, :])
            for n in range(packs):
                part = pl.ds(ROWS * n, ROWS)
                pr[side, part, :] = FY[side] * (ps[side, part, :] - pr[side, part, :])

    def shared(xr, xj, low, high, lj):
        result = jnp.where(row == 0, xr[0, pl.ds(xj, 1), :], 0.0)
        result = jnp.where(row == ROWS - 1, xr[1, pl.ds(xj, 1), :], result)
        result = result + jnp.where(lane == 0, pltpu.roll(low, lax.rem(LANES - lj, LANES), 1), 0.0)
        return result + jnp.where(lane == LANES - 1, pltpu.roll(high, LANES - 1 - lj, 1), 0.0)

    def shared_energy(xs, ps, first, pack, start, xr, pr, xr_first, pr_pack, pr_start):
        total = blank
        for side in range(2):
            for n in range(2 * NZ // ROWS):
                mine = xs[side, pl.ds(2 * NZ * first + ROWS * n, ROWS), :]
                total = total + mine * xr[side, pl.ds(2 * NZ * xr_first + ROWS * n, ROWS), :]
            mine = ps[side, pl.ds(ROWS * pack, ROWS), :]
            theirs = pr[side, pl.ds(ROWS * pr_pack, ROWS), :]
            if start != pr_start:
                mine = pltpu.roll(mine, (pr_start - start) % LANES, 1)
            inside = (lane >= pr_start) & (lane < pr_start + 2 * NZ)
            total = total + jnp.where(inside, mine * theirs, 0.0)
        return total

    for copy in halo1:
        copy.wait_recv()
    exchange(xs1, xr1, ps1, pr1, 2, 1)
    low1, high1 = pr1[0], pr1[1]

    def middle_rise(k, carry):
        pq0, paa, main, extra = carry
        w = complete(k, S0, xr1, low1, high1, 0, 0)
        wa = complete(k, SA, xr1, low1, high1, 2, 2 * NZ)
        pq0 = against(Z0, k, w, pq0)
        paa = against(ZA, k, wa, paa)
        main = rise(k, w[0], w[1], main, S0)
        extra = rise(k, wa[0], wa[1], extra, SA)
        return pq0, paa, main, extra

    triple = (blank, blank, blank)
    pq0, paa, main, extra = blocked_loop(NZ, middle_rise, (blank, blank, triple, triple))
    g0, gaa = main[2], extra[2]
    seed_b0, seed_b1 = load * S0[0, NZ], load * S0[1, NZ]

    def fall_second(i, carry):
        k = NZ - 1 - i
        g0, g1, h0, h1, b0, b1, low1, high1, low2, high2 = carry
        z0, z1, g0, g1 = fall(k, g0, g1, S0)
        a0, a1, h0, h1 = fall(k, h0, h1, SA)
        y0, y1, b0, b1 = fall_bare(k, b0, b1, ZB)
        packed = (low1, high1)
        for n, value in enumerate((y0, y1, z0, z1)):
            pack_rows(xs2, value, k + NZ * n)
            packed = pack_lane(packed, value, k + NZ * n)
        other = (low2, high2)
        for n, value in enumerate((a0, a1)):
            pack_rows(xs2, value, k + NZ * (n + 4))
            other = pack_lane(other, value, k + NZ * n)
        return (g0, g1, h0, h1, b0, b1) + packed + other

    carry = blocked_loop(
        NZ, fall_second, (blank, blank, blank, blank, seed_b0, seed_b1, blank, blank, blank, blank)
    )
    for n in range(2):
        ps2[0, ROWS * n : ROWS * (n + 1), :] = carry[6 + 2 * n]
        ps2[1, ROWS * n : ROWS * (n + 1), :] = carry[7 + 2 * n]
    halo2 = send_halo(2, xs2, xr2, ps2, pr2)
    rab = seed_a0 * ZB[0, NZ] + seed_a1 * ZB[1, NZ]
    rbb = seed_b0 * ZB[0, NZ] + seed_b1 * ZB[1, NZ]

    def inner_second(k, carry):
        d0, daa = carry
        weights = weights_of(k)
        keep(k, weights, ZB, SB)
        d0 = against(S0, k, operate(k, weights, S0), d0)
        daa = against(SA, k, operate(k, weights, SA), daa)
        return d0, daa

    d0, daa = blocked_loop(NZ, inner_second, (blank, blank))
    for copy in halo2:
        copy.wait_recv()
    exchange(xs2, xr2, ps2, pr2, 3, 2)
    low2, high2 = pr2[0, :ROWS, :], pr2[1, :ROWS, :]

    def last_rise(k, carry):
        pab, pbb, gab, main = carry
        w = complete(k, SB, xr2, low2, high2, 0, 0)
        pab = against(ZA, k, w, pab)
        pbb = against(ZB, k, w, pbb)
        gab = against(SA, k, w, gab)
        main = rise(k, w[0], w[1], main, SB)
        return pab, pbb, gab, main

    pab, pbb, gab, main = blocked_loop(NZ, last_rise, (blank, blank, blank, triple))
    gbb = main[2]

    def fall_third(i, carry):
        k = NZ - 1 - i
        g0, g1, low, high = carry
        z0, z1, g0, g1 = fall(k, g0, g1, SB)
        packed = (low, high)
        for n, value in enumerate((z0, z1)):
            pack_rows(xs3, value, k + NZ * n)
            packed = pack_lane(packed, value, k + NZ * n)
        return (g0, g1) + packed

    carry = blocked_loop(NZ, fall_third, (blank, blank, blank, blank))
    ps3[0] = carry[2]
    ps3[1] = carry[3]
    halo3 = send_halo(3, xs3, xr3, ps3, pr3)

    finals = []
    rest = []
    places = [
        gathered.at[0, :, :, my_rows, :],
        gathered.at[1, :, :, my_rows, :],
        adj.at[:, :, my_rows, :],
        hess.at[my_rows, :],
    ]

    def give_back(n, field):
        for o in range(1, ngz):
            send_back(n, o, field.at[:, pl.ds(1 + gzs[o] * depth, depth)])
        copy = pltpu.make_async_copy(field.at[:, pl.ds(1 + base, depth)], places[n], loc_sem.at[n])
        copy.start()
        finals.append(copy)

    def send_back(n, o, src):
        copy = pltpu.make_async_remote_copy(
            src_ref=src, dst_ref=places[n],
            send_sem=out_send.at[n, o], recv_sem=out_recv.at[n, o],
            device_id=peers[o - 1], device_id_type=MESH,
        )
        copy.start()
        rest.append(copy)

    give_back(0, Z0)
    give_back(1, S0)
    d0 = d0 + shared_energy(xs2, ps2, 1, 0, 2 * NZ, xr2, pr2, 1, 0, 2 * NZ)
    daa = daa + shared_energy(xs2, ps2, 2, 1, 0, xr2, pr2, 2, 1, 0)

    stages = ((group_a, ra, red_recv_a, ma), (group_b, rb, red_recv_b, mb))

    def gather_sums(values):
        for n, value in enumerate(values):
            stack[n : n + 1, :] = jnp.sum(value, axis=0, keepdims=True)
        each = jnp.sum(stack[...], axis=1, keepdims=True)
        return jnp.sum(jnp.where(lane == row, each, 0.0), axis=0, keepdims=True)

    def send_sum(stage, value):
        rt[stage] = value
        group, received, sem, place = stages[stage]
        received[place] = value
        copies = []
        for o, device in enumerate(group):
            copy = pltpu.make_async_remote_copy(
                src_ref=rt.at[stage], dst_ref=received.at[place],
                send_sem=red_send.at[stage, o], recv_sem=sem.at[o],
                device_id=device, device_id_type=MESH,
            )
            copy.start()
            copies.append(copy)
        return copies

    def finish_sum(stage, copies):
        for copy in copies:
            copy.wait_recv()
        return jnp.sum(stages[stage][1][...], axis=0)

    def spread(total, count):
        each = jnp.sum(jnp.where(lane == row, total, 0.0), axis=1, keepdims=True)
        each = jnp.broadcast_to(each, (ROWS, LANES))
        return [each[n : n + 1, :] for n in range(count)]


    def inner_third(k, carry):
        dab, dbb = carry
        image = operate(k, weights_of(k), SB)
        return against(SA, k, image, dab), against(SB, k, image, dbb)

    dab, dbb = blocked_loop(NZ, inner_third, (blank, blank))
    for copy in halo3:
        copy.wait_recv()
    exchange(xs3, xr3, ps3, pr3, 1, 1)
    dab = dab + shared_energy(xs2, ps2, 2, 1, 0, xr3, pr3, 0, 0, 0)
    dbb = dbb + shared_energy(xs3, ps3, 0, 0, 0, xr3, pr3, 0, 0, 0)
    sums = [rz0, pq0, g0, d0, raa, rab, rbb, paa, pab, pbb, gaa, gab, gbb, daa, dab, dbb]
    first = send_sum(0, gather_sums(sums))
    second = send_sum(1, finish_sum(0, first))
    reductions = first + second
    (rz0, pq0, g0, d0, raa, rab, rbb, paa, pab, pbb, gaa, gab, gbb, daa, dab, dbb) = spread(finish_sum(1, second), 16)

    def combination(rz, pq, g, d):
        step = rz / pq
        renewed = step * step * g - rz
        grow = 1.0 + renewed / rz
        energy = grow * grow * pq - 2.0 * grow * step * g + step * step * d
        second = renewed / energy
        return step + second * grow, -(second * step)

    c0, c1 = combination(rz0, pq0, g0, d0)

    def form(aa, ab, bb):
        return c0 * c0 * aa + 2.0 * (c0 * c1) * ab + c1 * c1 * bb

    e0, e1 = combination(form(raa, rab, rbb), form(paa, pab, pbb), form(gaa, gab, gbb), form(daa, dab, dbb))
    f_za, f_zb, f_sa, f_sb = e0 * c0, e0 * c1, e1 * c0, e1 * c1

    def adjoints(k, carry):
        level = jnp.full((ROWS, LANES), k, jnp.int32).astype(F32)
        at = level == kbed
        out = []
        for c in range(2):
            value = (f_za * ZA[c, k + 1] + f_zb * ZB[c, k + 1]) + (f_sa * SA[c, k + 1] + f_sb * SB[c, k + 1])
            ZA[c, k + 1] = value
            out.append(jnp.where(at, value, carry[c]))
        return tuple(out)

    landed = len(rest)
    basal = (blank, blank)
    for o in (*range(1, ngz), 0):
        for k in range(depth):
            basal = adjoints(gzs[o] * depth + k, basal)
        if o:
            send_back(2, o, ZA.at[:, pl.ds(1 + gzs[o] * depth, depth)])
    own = pltpu.make_async_copy(ZA.at[:, pl.ds(1 + base, depth)], places[2], loc_sem.at[2])
    own.start()
    finals.append(own)
    action = friction * (speed0 * basal[0] + speed1 * basal[1])
    hess[my_rows, :] = action
    vbs[0, my_rows, :] = action
    for o in range(1, ngz):
        send_back(3, o, vbs.at[0, my_rows, :])
    for copy in finals[:2]:
        copy.wait()
    for copy in rest[:landed]:
        copy.wait_recv()

    def increments(k, carry):
        for c in range(2):
            gathered[0, c, k] = c0 * gathered[0, c, k] + c1 * gathered[1, c, k]
        return carry

    lax.fori_loop(0, depth, increments, 0)
    final = pltpu.make_async_copy(gathered.at[0], inc, loc_sem.at[3])
    final.start()

    for copy in finals[2:] + [final]:
        copy.wait()
    for copy in rest[landed:]:
        copy.wait_recv()
    for copy in rest:
        copy.wait_send()
    for group in incoming:
        for copy in group:
            copy.wait_send()
    for copy in halo0 + halo1 + halo2 + halo3 + reductions:
        copy.wait_send()


def deliver(inc_in, adj_in, hess_in, inc, adj, hess, first, second, third, sem):
    held = [(inc_in.at[c], first.at[c], inc.at[c]) for c in range(2)]
    held += [(adj_in.at[c], second.at[c], adj.at[c]) for c in range(2)]
    held += [(hess_in, third, hess)]
    reads = [pltpu.make_async_copy(src, mid, sem.at[n, 0]) for n, (src, mid, _) in enumerate(held)]
    writes = [pltpu.make_async_copy(mid, dst, sem.at[n, 1]) for n, (_, mid, dst) in enumerate(held)]
    for copy in reads:
        copy.start()
    for read, write in zip(reads, writes):
        read.wait()
        write.start()
    for copy in writes:
        copy.wait()


def local(sizes, *args):
    ngx, ngy, ngz = sizes
    field = pltpu.VMEM((NZ, ROWS, LANES), F32)
    state = pltpu.VMEM((2, NZ + 2, ROWS, LANES), F32)
    depth, rows, lanes = args[1].shape
    dma = pltpu.SemaphoreType.DMA

    def halo(length, packs):
        return [pltpu.VMEM((2, length, LANES), F32)] * 2 + [pltpu.VMEM((2, packs * ROWS, LANES), F32)] * 2

    na, nb = ngx * 2, (ngy // 2) * ngz
    scratch = (
        [pltpu.VMEM((2, depth, rows, lanes), F32), pltpu.VMEM((rows, lanes), jnp.int32)]
        + [pltpu.VMEM((ROWS, LANES), F32)] * 3
        + [pltpu.VMEM((2, 2 * NZ, LANES), F32)]
        + [pltpu.VMEM((NZ + 1, ROWS, LANES), F32), pltpu.VMEM((3, NZ, ROWS, LANES), F32), field]
        + [pltpu.VMEM((2, rows, lanes), F32), pltpu.VMEM((ngz, 2, ROWS, LANES), F32)]
        + [pltpu.VMEM((NZ + 1, ROWS, LANES), F32)]
        + [field] * 6
        + [state] * 6
        + halo(NZ + 8, 1) + halo(4 * NZ, 1) + halo(6 * NZ, 2) + halo(2 * NZ, 1)
        + [pltpu.VMEM((ROWS, LANES), F32), pltpu.VMEM((2, 1, LANES), F32)]
        + [pltpu.VMEM((na, 1, LANES), F32), pltpu.VMEM((nb, 1, LANES), F32)]
        + [pltpu.VMEM((2, 2, depth, rows, lanes), F32)]
        + [dma((5,)), dma((4,)), dma((4, ngz)), dma((4, ngz)), dma((4, 4)), dma((4, 4))]
        + [dma((2, max(na, nb))), dma((na,)), dma((nb,)), dma((4, ngz)), dma((4, ngz))]
    )
    vmem = pl.BlockSpec(memory_space=pltpu.VMEM)
    hbm = pl.BlockSpec(memory_space=pl.ANY)
    smem = pl.BlockSpec(memory_space=pltpu.SMEM)
    shapes = (
        jax.ShapeDtypeStruct((2, depth, rows, lanes), F32),
        jax.ShapeDtypeStruct((2, depth, rows, lanes), F32),
        jax.ShapeDtypeStruct((rows, lanes), F32),
    )
    results = pl.pallas_call(
        functools.partial(kernel, sizes),
        out_shape=shapes,
        in_specs=[hbm] * 7 + [smem, hbm],
        out_specs=(hbm, hbm, vmem),
        scratch_shapes=scratch,
        compiler_params=pltpu.CompilerParams(
            collective_id=0, has_side_effects=True, vmem_limit_bytes=62 * 1024 * 1024
        ),
    )(*args)
    return pl.pallas_call(
        deliver,
        out_shape=shapes,
        in_specs=[hbm] * 3,
        out_specs=(hbm, hbm, hbm),
        scratch_shapes=[pltpu.VMEM(shape.shape, F32) for shape in shapes] + [dma((5, 2))],
        compiler_params=pltpu.CompilerParams(vmem_limit_bytes=62 * 1024 * 1024),
    )(*results)


def solution(mesh):
    sizes = (mesh.shape["gx"], mesh.shape["gy"], mesh.shape["gz"])
    wide, cell, flat = P(None, "gz", "gx", "gy"), P("gz", "gx", "gy"), P("gx", "gy")
    return jax.shard_map(
        functools.partial(local, sizes),
        mesh=mesh,
        in_specs=(wide, cell, wide, cell, flat, flat, flat, flat, flat),
        out_specs=(wide, wide, flat),
        check_vma=False,
    )
```
